256 devices in a mesh: pipe: 8 (over y, x_lo), expert: 32 (over x_hi, z, core).
Axes of the slice: x: 4 (x_hi: 2, x_lo: 2; x = x_hi * 2 + x_lo), y: 4, z: 8, core: 2. Of those that a mesh axis runs over, the one named last changes fastest.
Arguments:
- acts_a: bfloat16 [8, 2048, 7168], P('pipe', 'expert'), may hold values from -6 to 6
- acts_b: bfloat16 [8, 2048, 7168], P('pipe', 'expert'), may hold values from -6 to 6
- cot_b: bfloat16 [8, 2048, 7168], P('pipe', 'expert'), may hold values from -1.5 to 1.5
- routes_a: int32 [8, 2048, 2], P('pipe', 'expert'), may hold values from 0 to 3, all different within a row; in each aligned block of 64 rows (0 to 63, 64 to 127, ..., all dimensions but the last counted through in order) at most 34 rows name the same one
- gates_a: float32 [8, 2048, 2], P('pipe', 'expert'), may hold values from 0.1 to 1
- routes_b: int32 [8, 2048, 2], P('pipe', 'expert'), may hold values from 0 to 3, all different within a row; in each aligned block of 64 rows (0 to 63, 64 to 127, ..., all dimensions but the last counted through in order) at most 34 rows name the same one
- gates_b: float32 [8, 2048, 2], P('pipe', 'expert'), may hold values from 0.1 to 1
- up_weight: bfloat16 [8, 28672, 1024], P('pipe', 'expert'), may hold values from -0.0625 to 0.0625
- down_weight: bfloat16 [8, 1024, 28672], P('pipe', None, 'expert'), may hold values from -0.1875 to 0.1875
- up_scale: float32 [8, 4], P('pipe'), may hold values from 0.002362278 to 0.004724556
- down_scale: float32 [8, 4], P('pipe'), may hold values from 0.00625 to 0.0125
Outputs:
- next_a: bfloat16 [8, 2048, 7168], P('pipe', 'expert')
- next_cot_b: bfloat16 [8, 2048, 7168], P('pipe', 'expert')
- up_grad: bfloat16 [8, 28672, 1024], P('pipe', 'expert')
- down_grad: bfloat16 [8, 1024, 28672], P('pipe', None, 'expert')
- up_scale_grad: float32 [8, 4], P('pipe')
- down_scale_grad: float32 [8, 4], P('pipe')
The draws below stay inside these ranges and needn't reach their ends.
Inputs may be any that keep to these rules, and one draw needn't show every extreme that they name: `routes_a`: within the rows of one device no expert is chosen by more than 34 rows, and some expert is chosen by exactly 34 rows there. `routes_b`: within the rows of one device no expert is chosen by more than 34 rows, and some expert is chosen by exactly 34 rows there.
All inputs are finite; a program needn't handle non-finite values.
Results may differ from the reference program's by a relative error of at most 0.0091.
Values may be sent and summed in bfloat16 or wider, within the bound.
A program may use at most 128 MiB of HBM per device.

```python
import math
import jax
import jax.numpy as jnp
import numpy as np
from jax import lax

D = 7168
HID = 1024
EXPERTS = 4
TOP = 2
TOK_DEV = 64
TOKENS = 2048
CAP = 34
N_PIPE = 8
N_EXPERT = 32


def level_of(own_key, extent, split, smallest, top_value):
    gain = 1.0
    for dim, parts in split:
        heights = jax.random.uniform(jax.random.fold_in(jax.random.fold_in(own_key, 6), dim), (parts,), jnp.float32, smallest / len(split), top_value / len(split))
        gain = gain * jnp.repeat(jnp.exp(heights), extent[dim] // parts).reshape((-1,) + (1,) * (len(extent) - 1 - dim))
    return gain


def assign_block(own_key, own, number, rows, count, top, most, lean):
    order = jax.random.permutation(own_key, count)
    crowded, common = load_shares(count, rows * top, most, lean, True), load_shares(count, rows * top, most, lean, False)
    places = jnp.arange(count)

    def named(lengths, offset_by):
        used = int((lengths > 0).sum())
        fixed = max(1, used // 4)
        passed = fixed + (places - fixed + offset_by * (used - fixed)) % max(1, count - fixed)
        return jnp.zeros((count,), jnp.int32).at[order[jnp.where(places < fixed, places, passed)]].set(jnp.asarray(lengths, jnp.int32))

    lengths = jnp.where(number % 4 == 0, named(crowded, number // 4), named(common, number - number // 4 - 1))
    mixed = jax.random.permutation(jax.random.fold_in(own, 3), count)
    donor, sink = mixed[0:count // 2 * 2:2], mixed[1:count // 2 * 2:2]
    room = jnp.minimum(lengths[donor] - 1, most - lengths[sink]) // 2
    room = jnp.where((donor == order[0]) | (sink == order[0]) | (lengths[sink] == 0), 0, jnp.maximum(room, 0))
    passed = jax.random.randint(jax.random.fold_in(own, 4), (count // 2,), 0, 1 << 20) % (room + 1)
    lengths = lengths.at[donor].add(-passed).at[sink].add(passed)
    members = jnp.searchsorted(jnp.cumsum(lengths), jnp.arange(rows * top), side="right").astype(jnp.int32)
    table = members.reshape(top, rows).T
    table = table[jax.random.permutation(jax.random.fold_in(own, 1), rows)]
    offset_by = jax.random.randint(jax.random.fold_in(own, 2), (rows, 1), 0, top)
    return jnp.take_along_axis(table, (jnp.arange(top)[None, :] + offset_by) % top, axis=1)


def load_shares(amount, total, limit, skew, full):
    weights = [(1 << 20) // math.isqrt(standing ** skew) + 1 for standing in range(1, amount + 1)]
    largest = limit if full else min(limit, max(-(-total // amount), total * weights[0] // sum(weights)))
    least = 1 if total - largest >= amount - 1 else 0
    given, rest = [largest] + [least] * (amount - 1), total - largest - least * (amount - 1)
    while rest > 0:
        free = [i for i in range(1, amount) if given[i] < largest] or [i for i in range(1, amount) if given[i] < limit]
        pool, remaining = sum([weights[i] for i in free]), rest
        for i in free:
            addition = min(limit - given[i], max(1, remaining * weights[i] // pool), rest)
            given[i] = given[i] + addition
            rest = rest - addition
    return np.array(given)


def noise(stream_key, extent, deviation, reach, cuts=(), held_as=jnp.bfloat16):
    values = jax.random.normal(stream_key, extent, jnp.float32) * deviation
    if len(cuts) > 0:
        values = level_of(stream_key, extent, cuts, -0.22, 0.18) * values
    return jnp.clip(values, min=-reach, max=reach).astype(held_as)


def setup_inputs(seed: int = 0) -> dict:
    arg_keys = jax.random.split(jax.random.key(seed), 12)
    acts_a = noise(arg_keys[0], (N_PIPE, TOKENS, D), 1.0, 6.0, ((0, 8), (1, 32)))
    acts_b = noise(arg_keys[1], (N_PIPE, TOKENS, D), 1.0, 6.0, ((0, 8), (1, 32)))
    cot_b = noise(arg_keys[2], (N_PIPE, TOKENS, D), 0.25, 1.5, ((0, 8), (1, 32)))
    routes_a_keys = jax.random.split(jax.random.fold_in(arg_keys[3], 1), N_PIPE * TOKENS // TOK_DEV)
    routes_a_turns = jax.random.permutation(jax.random.fold_in(arg_keys[3], 3), N_PIPE * TOKENS // TOK_DEV)
    routes_a = jax.vmap(lambda own, number: assign_block(jax.random.fold_in(arg_keys[3], 2), own, number, TOK_DEV, EXPERTS, TOP, CAP, 2))(routes_a_keys, routes_a_turns).reshape((N_PIPE, TOKENS, TOP))
    gates_a = jnp.clip(0.1 + 0.9 * jax.random.uniform(arg_keys[4], (N_PIPE, TOKENS, TOP), jnp.float32) ** level_of(arg_keys[4], (N_PIPE, TOKENS, TOP), ((0, 8), (1, 32)), -0.2, 0.2), 0.1, 1.0)
    routes_b_keys = jax.random.split(jax.random.fold_in(arg_keys[5], 1), N_PIPE * TOKENS // TOK_DEV)
    routes_b_turns = jax.random.permutation(jax.random.fold_in(arg_keys[5], 3), N_PIPE * TOKENS // TOK_DEV)
    routes_b = jax.vmap(lambda own, number: assign_block(jax.random.fold_in(arg_keys[5], 2), own, number, TOK_DEV, EXPERTS, TOP, CAP, 2))(routes_b_keys, routes_b_turns).reshape((N_PIPE, TOKENS, TOP))
    gates_b = jnp.clip(0.1 + 0.9 * jax.random.uniform(arg_keys[6], (N_PIPE, TOKENS, TOP), jnp.float32) ** level_of(arg_keys[6], (N_PIPE, TOKENS, TOP), ((0, 8), (1, 32)), -0.2, 0.2), 0.1, 1.0)
    up_weight = noise(arg_keys[7], (N_PIPE, EXPERTS * D, HID), D ** -0.5, 0.0625, ((0, 8), (1, 32)))
    down_weight = noise(arg_keys[8], (N_PIPE, HID, EXPERTS * D), HID ** -0.5, 0.1875, ((0, 8), (2, 32)))
    up_scale = jnp.clip(jnp.exp(math.log(0.004724556) - 0.6931472 * jax.random.uniform(arg_keys[9], (N_PIPE, EXPERTS), jnp.float32) ** level_of(arg_keys[9], (N_PIPE, EXPERTS), ((0, 8),), -0.2, 0.2)), 0.002362278, 0.004724556)
    down_scale = jnp.clip(jnp.exp(math.log(0.0125) - 0.6931472 * jax.random.uniform(arg_keys[10], (N_PIPE, EXPERTS), jnp.float32) ** level_of(arg_keys[10], (N_PIPE, EXPERTS), ((0, 8),), -0.2, 0.2)), 0.00625, 0.0125)
    return dict(acts_a=acts_a, acts_b=acts_b, cot_b=cot_b, routes_a=routes_a, gates_a=gates_a, routes_b=routes_b, gates_b=gates_b, up_weight=up_weight, down_weight=down_weight, up_scale=up_scale, down_scale=down_scale)


qlimit = 7.0
epsilon = 1e-06
two_pi = 2.0 * math.pi
highest = lax.Precision.HIGHEST

def rms_norm(values):
    return values * lax.rsqrt(lax.optimization_barrier(jnp.mean(values * values, axis=-1, keepdims=True)) + epsilon)

def soft_round(values):
    return values - jnp.sin(two_pi * values) / two_pi

def fake_quant(weights, scale):
    ratio = weights.astype(jnp.float32) / scale
    return scale * soft_round(jnp.clip(ratio, -qlimit, qlimit))

def quant_grads(weights, scale, grads):
    ratio = weights.astype(jnp.float32) / scale
    inside = jnp.abs(ratio) < qlimit
    wave = 1.0 - jnp.cos(two_pi * ratio)
    grads_wide = grads.astype(jnp.float32)
    weight_grad = grads_wide * jnp.where(inside, wave, 0.0)
    slope = soft_round(jnp.clip(ratio, -qlimit, qlimit)) - jnp.where(inside, ratio * wave, 0.0)
    scale_grad = lax.optimization_barrier(jnp.sum(grads_wide * slope, axis=(1, 2))) / math.sqrt(D * HID * qlimit)
    return (weight_grad, scale_grad)

def silu_grad(values):
    sigma_v = jax.nn.sigmoid(values)
    return sigma_v * (1.0 + values * (1.0 - sigma_v))

def route_tables(routes, gates):
    flat_ids = routes.reshape(-1)
    entries = flat_ids.shape[0]
    chosen = routes.shape[1]
    matches = (flat_ids[:, None] == jnp.arange(EXPERTS, dtype=jnp.int32)[None, :]).astype(jnp.int32)
    before = jnp.cumsum(matches, axis=0) - matches
    slot_of = lax.optimization_barrier(jnp.sum(before * matches, axis=1))
    at_slot = (slot_of[:, None] == jnp.arange(CAP, dtype=jnp.int32)[None, :]).astype(jnp.float32)
    owner_of = ((jnp.arange(entries, dtype=jnp.int32) // chosen)[:, None] == jnp.arange(routes.shape[0], dtype=jnp.int32)[None, :]).astype(jnp.float32)
    matches_wide = matches.astype(jnp.float32)
    dispatch = jnp.einsum('re,rc,rt->ect', matches_wide, at_slot, owner_of, precision=highest)
    weighted = jnp.einsum('re,rc,rt->ect', matches_wide * gates.reshape(-1)[:, None].astype(jnp.float32), at_slot, owner_of, precision=highest)
    return (dispatch, weighted)

def gather_rows(values, table):
    packed = jnp.einsum('nect,ntd->encd', table, values.astype(jnp.float32), precision=highest)
    return packed.astype(jnp.bfloat16).reshape(EXPERTS, N_EXPERT * CAP, D)

def scatter_rows(rows, table):
    shaped = rows.astype(jnp.float32).reshape(EXPERTS, N_EXPERT, CAP, D)
    return jnp.einsum('nect,encd->ntd', table, shaped, precision=highest)

def reference(acts_a, acts_b, cot_b, routes_a, gates_a, routes_b, gates_b, up_weight, down_weight, up_scale, down_scale):
    tables = jax.vmap(route_tables)
    empty = jnp.zeros((TOKENS, D), jnp.bfloat16)
    forward_out = [empty]
    backward_out = [empty for index in range(N_PIPE)]
    up_grads, down_grads, up_sgrads, down_sgrads = ([], [], [], [])
    for section in range(N_PIPE):
        up_blocks = up_weight[section].reshape(EXPERTS, D, HID)
        down_blocks = down_weight[section].reshape(HID, EXPERTS, D).transpose(1, 0, 2)
        up_steps = up_scale[section][:, None, None]
        down_steps = down_scale[section][:, None, None]
        q_up = fake_quant(up_blocks, up_steps).astype(jnp.bfloat16).astype(jnp.float32)
        q_down = fake_quant(down_blocks, down_steps).astype(jnp.bfloat16).astype(jnp.float32)
        x_a = acts_a[section].astype(jnp.float32).reshape(N_EXPERT, TOK_DEV, D)
        normed_a = rms_norm(x_a).astype(jnp.bfloat16)
        disp_a, comb_a = tables(routes_a[section].reshape(N_EXPERT, TOK_DEV, TOP), gates_a[section].reshape(N_EXPERT, TOK_DEV, TOP))
        rows_a = gather_rows(normed_a, disp_a).astype(jnp.float32)
        pre_a = jnp.einsum('erd,edh->erh', rows_a, q_up).astype(jnp.bfloat16)
        hidden_a = jax.nn.silu(pre_a.astype(jnp.float32)).astype(jnp.bfloat16)
        expert_a = jnp.einsum('erh,ehd->erd', hidden_a.astype(jnp.float32), q_down).astype(jnp.bfloat16)
        mixed = (x_a + scatter_rows(expert_a, comb_a)).astype(jnp.bfloat16).reshape(TOKENS, D)
        if section + 1 < N_PIPE:
            forward_out.append(mixed)
        x_b = acts_b[section].astype(jnp.float32).reshape(N_EXPERT, TOK_DEV, D)
        cot_here = cot_b[section].astype(jnp.float32).reshape(N_EXPERT, TOK_DEV, D)
        normed_wide, norm_back = jax.vjp(rms_norm, x_b)
        disp_b, comb_b = tables(routes_b[section].reshape(N_EXPERT, TOK_DEV, TOP), gates_b[section].reshape(N_EXPERT, TOK_DEV, TOP))
        rows_b = gather_rows(normed_wide.astype(jnp.bfloat16), disp_b).astype(jnp.float32)
        cots_b = gather_rows(cot_here, comb_b).astype(jnp.float32)
        pre_b = jnp.einsum('erd,edh->erh', rows_b, q_up).astype(jnp.bfloat16).astype(jnp.float32)
        hidden_b = jax.nn.silu(pre_b).astype(jnp.bfloat16).astype(jnp.float32)
        hidden_grad = jnp.einsum('erd,ehd->erh', cots_b, q_down).astype(jnp.bfloat16).astype(jnp.float32)
        pre_grad = (hidden_grad * silu_grad(pre_b)).astype(jnp.bfloat16).astype(jnp.float32)
        input_rows = jnp.einsum('erh,edh->erd', pre_grad, q_up).astype(jnp.bfloat16)
        up_gq = jnp.einsum('erd,erh->edh', rows_b, pre_grad).astype(jnp.bfloat16)
        down_gq = jnp.einsum('erh,erd->ehd', hidden_b, cots_b).astype(jnp.bfloat16)
        back_b, = norm_back(scatter_rows(input_rows, disp_b))
        grad_in = (cot_here + back_b).astype(jnp.bfloat16).reshape(TOKENS, D)
        if section > 0:
            backward_out[section - 1] = grad_in
        up_w, up_s = quant_grads(up_blocks, up_steps, up_gq)
        down_w, down_s = quant_grads(down_blocks, down_steps, down_gq)
        up_grads.append(up_w.reshape(EXPERTS * D, HID).astype(jnp.bfloat16))
        down_grads.append(down_w.transpose(1, 0, 2).reshape(HID, EXPERTS * D).astype(jnp.bfloat16))
        up_sgrads.append(up_s)
        down_sgrads.append(down_s)
    return (jnp.stack(forward_out), jnp.stack(backward_out), jnp.stack(up_grads), jnp.stack(down_grads), jnp.stack(up_sgrads), jnp.stack(down_sgrads))
```

```python
import math

import jax
import jax.numpy as jnp
from jax import lax
from jax.sharding import PartitionSpec as P

D = 7168
HID = 1024
EXPERTS = 4
CAP = 34


qlimit = 7.0
epsilon = 1e-06
two_pi = 2.0 * math.pi
highest = lax.Precision.HIGHEST


def partner_2(value, axis, bit):
    return lax.ppermute(value, axis, [(i, i ^ 1 << bit) for i in range(lax.axis_size(axis))])


def passed_along(value, axis, by):
    peers = lax.axis_size(axis)
    pairs = [(i, i + by) for i in range(peers) if 0 <= i + by < peers]
    return lax.ppermute(value, axis, pairs)


def rms_norm(values):
    return values * lax.rsqrt(jnp.mean(values * values, axis=-1, keepdims=True) + epsilon)


SIN_PI = (3.1415927410125732, -5.167710304260254, 2.550077438354492, -0.598291277885437, 0.07765766233205795)
COS_PI = (
    1.0,
    -4.934802055358887,
    4.058709144592285,
    -1.335211992263794,
    0.23493731021881104,
    -0.024396324530243874,
)


def poly(coefs, square):
    total = coefs[-1]
    for coef in coefs[-2::-1]:
        total = total * square + coef
    return total


def half_waves(values):
    rest = values - jnp.round(values)
    square = rest * rest
    return (rest * poly(SIN_PI, square), poly(COS_PI, square))


def fake_quant(weights, inverse, scale):
    ratio = jnp.clip(weights.astype(jnp.float32) * inverse, -qlimit, qlimit)
    sine, cosine = half_waves(ratio)
    return scale * (ratio - sine * cosine * (1.0 / math.pi))


def quant_grads(weights, inverse, grads):
    ratio = weights.astype(jnp.float32) * inverse
    inside = jnp.abs(ratio) < qlimit
    clipped = jnp.clip(ratio, -qlimit, qlimit)
    sine, cosine = half_waves(clipped)
    wave = jnp.where(inside, 2.0 * sine * sine, 0.0)
    grads_wide = grads.astype(jnp.float32)
    slope = clipped - sine * cosine * (1.0 / math.pi) - clipped * wave
    scale_grad = jnp.sum(grads_wide * slope) / math.sqrt(D * HID * qlimit)
    return (grads_wide * wave, scale_grad)


def silu_grad(values):
    sigma_v = jax.nn.sigmoid(values)
    return sigma_v * (1.0 + values * (1.0 - sigma_v))


def route_tables(routes, gates):
    flat_ids = routes.reshape(-1)
    entries = flat_ids.shape[0]
    chosen = routes.shape[1]
    matches = (flat_ids[:, None] == jnp.arange(EXPERTS, dtype=jnp.int32)[None, :]).astype(jnp.int32)
    order = jnp.arange(entries, dtype=jnp.int32)
    earlier = (order[:, None] > order[None, :]).astype(jnp.float32)
    before = jnp.dot(earlier, matches.astype(jnp.float32), precision=highest).astype(jnp.int32)
    slot_of = jnp.sum(before * matches, axis=1)
    at_slot = (slot_of[:, None] == jnp.arange(CAP, dtype=jnp.int32)[None, :]).astype(jnp.float32)
    owner_of = (
        (jnp.arange(entries, dtype=jnp.int32) // chosen)[:, None]
        == jnp.arange(routes.shape[0], dtype=jnp.int32)[None, :]
    ).astype(jnp.float32)
    matches_wide = matches.astype(jnp.float32)
    dispatch = jnp.einsum("re,rc,rt->ect", matches_wide, at_slot, owner_of, precision=highest)
    weighted = jnp.einsum(
        "re,rc,rt->ect",
        matches_wide * gates.reshape(-1)[:, None],
        at_slot,
        owner_of,
        precision=highest,
    )
    return (dispatch, weighted)


def pack_rows(values, table, split_count):
    shaped = values.reshape(values.shape[0], split_count, -1)
    packed = jnp.einsum(
        "ect,tsd->escd", table.astype(jnp.bfloat16), shaped, preferred_element_type=jnp.float32
    )
    return packed.astype(jnp.bfloat16).reshape(EXPERTS * split_count, CAP, -1)


def pack_scaled(values, table, split_count):
    shaped = values.astype(jnp.float32).reshape(values.shape[0], split_count, -1)
    packed = jnp.einsum("ect,tsd->escd", table, shaped, precision=highest)
    return packed.astype(jnp.bfloat16).reshape(EXPERTS * split_count, CAP, -1)


def unpack_rows(returned, table, split_count):
    shaped = returned.astype(jnp.float32).reshape(EXPERTS, split_count, CAP, -1)
    summed = jnp.einsum("ect,escd->tsd", table, shaped, precision=highest)
    return summed.reshape(summed.shape[0], -1)


def shards(
    acts_a,
    acts_b,
    cot_b,
    routes_a,
    gates_a,
    routes_b,
    gates_b,
    up_weight,
    down_weight,
    up_scale,
    down_scale,
):
    split_count = lax.axis_size("expert") // EXPERTS
    split_bits = split_count.bit_length() - 1
    device_id = lax.axis_index("expert")
    expert_id = device_id // split_count
    part_id = device_id % split_count
    is_mine = (jnp.arange(EXPERTS, dtype=jnp.int32) == expert_id).astype(jnp.float32)
    s_up = jnp.sum(is_mine * up_scale[0])
    s_down = jnp.sum(is_mine * down_scale[0])
    w_up = up_weight[0]
    w_down = down_weight[0]
    inv_up = 1.0 / s_up
    inv_down = 1.0 / s_down
    q_up, q_down = lax.optimization_barrier(
        (
            fake_quant(w_up, inv_up, s_up).astype(jnp.bfloat16),
            fake_quant(w_down, inv_down, s_down).astype(jnp.bfloat16),
        )
    )
    part_width = w_up.shape[0]
    contract_last = (((1,), (1,)), ((), ()))
    contract_first = (((0,), (0,)), ((), ()))
    bit_order = list(range(split_bits))

    def part_sum(partial_value):
        current = partial_value
        for bit_no in bit_order:
            half_cols = current.shape[1] // 2
            upper_side = part_id >> bit_no & 1 == 1
            lower_part = current[:, :half_cols]
            upper_part = current[:, half_cols:]
            keep_part = jnp.where(upper_side, upper_part, lower_part)
            give_part = jnp.where(upper_side, lower_part, upper_part)
            given = partner_2(give_part.astype(jnp.bfloat16), "expert", bit_no)
            current = keep_part + given.astype(jnp.float32)
        current = current.astype(jnp.bfloat16)
        for bit_no in reversed(bit_order):
            partner = partner_2(current, "expert", bit_no)
            upper_side = part_id >> bit_no & 1 == 1
            current = jnp.concatenate(
                (jnp.where(upper_side, partner, current), jnp.where(upper_side, current, partner)),
                axis=1,
            )
        return current

    x_a = acts_a[0]
    normed_a = rms_norm(x_a.astype(jnp.float32)).astype(jnp.bfloat16)
    disp_a, comb_a = route_tables(routes_a[0], gates_a[0])
    arrived_a = lax.all_to_all(
        pack_rows(normed_a, disp_a, split_count), "expert", split_axis=0, concat_axis=0, tiled=True
    )
    rows_in = arrived_a.reshape(-1, part_width)
    pre_a = part_sum(jnp.dot(rows_in, q_up, preferred_element_type=jnp.float32))
    hidden_a = jax.nn.silu(pre_a.astype(jnp.float32)).astype(jnp.bfloat16)
    outputs = jnp.dot(hidden_a, q_down, preferred_element_type=jnp.float32).astype(jnp.bfloat16)
    returned_a = lax.all_to_all(
        outputs.reshape(arrived_a.shape), "expert", split_axis=0, concat_axis=0, tiled=True
    )
    out_a = (x_a.astype(jnp.float32) + unpack_rows(returned_a, comb_a, split_count)).astype(
        jnp.bfloat16
    )
    x_b = acts_b[0].astype(jnp.float32)
    normed_wide, norm_back = jax.vjp(rms_norm, x_b)
    disp_b, comb_b = route_tables(routes_b[0], gates_b[0])
    send_u = pack_rows(normed_wide.astype(jnp.bfloat16), disp_b, split_count)
    send_c = pack_scaled(cot_b[0], comb_b, split_count)
    arrived_u, arrived_c = (
        lax.all_to_all(send_u, "expert", split_axis=0, concat_axis=0, tiled=True),
        lax.all_to_all(send_c, "expert", split_axis=0, concat_axis=0, tiled=True),
    )
    rows_u = arrived_u.reshape(-1, part_width)
    rows_c = arrived_c.reshape(-1, part_width)
    pre_b = part_sum(jnp.dot(rows_u, q_up, preferred_element_type=jnp.float32))
    hidden_grad = part_sum(
        lax.dot_general(rows_c, q_down, contract_last, preferred_element_type=jnp.float32)
    )
    pre_wide = pre_b.astype(jnp.float32)
    hidden_b = jax.nn.silu(pre_wide).astype(jnp.bfloat16)
    pre_grad = (hidden_grad.astype(jnp.float32) * silu_grad(pre_wide)).astype(jnp.bfloat16)
    input_rows = lax.dot_general(
        pre_grad, q_up, contract_last, preferred_element_type=jnp.float32
    ).astype(jnp.bfloat16)
    g_up = lax.dot_general(
        rows_u, pre_grad, contract_first, preferred_element_type=jnp.float32
    ).astype(jnp.bfloat16)
    g_down = lax.dot_general(
        hidden_b, rows_c, contract_first, preferred_element_type=jnp.float32
    ).astype(jnp.bfloat16)
    input_rows, g_up, g_down = (input_rows.reshape(arrived_u.shape), g_up, g_down)
    returned_b = lax.all_to_all(input_rows, "expert", split_axis=0, concat_axis=0, tiled=True)
    (back_b,) = norm_back(unpack_rows(returned_b, disp_b, split_count))
    grad_in = (cot_b[0].astype(jnp.float32) + back_b).astype(jnp.bfloat16)
    next_a = passed_along(out_a, "pipe", 1)
    next_cot = passed_along(grad_in, "pipe", -1)
    dw_up, ds_up = quant_grads(w_up, inv_up, g_up)
    dw_down, ds_down = quant_grads(w_down, inv_down, g_down)
    sums = jnp.concatenate((is_mine * ds_up, is_mine * ds_down))
    for bit_no in range(lax.axis_size("expert").bit_length() - 1):
        sums = sums + partner_2(sums, "expert", bit_no)
    up_sums, down_sums = (sums[:EXPERTS], sums[EXPERTS:])
    return (
        next_a[None],
        next_cot[None],
        dw_up.astype(jnp.bfloat16)[None],
        dw_down.astype(jnp.bfloat16)[None],
        up_sums[None],
        down_sums[None],
    )


def solution(mesh):
    return jax.shard_map(
        shards,
        mesh=mesh,
        in_specs=(
            P("pipe", "expert", None),
            P("pipe", "expert", None),
            P("pipe", "expert", None),
            P("pipe", "expert", None),
            P("pipe", "expert", None),
            P("pipe", "expert", None),
            P("pipe", "expert", None),
            P("pipe", "expert", None),
            P("pipe", None, "expert"),
            P("pipe", None),
            P("pipe", None),
        ),
        out_specs=(
            P("pipe", "expert", None),
            P("pipe", "expert", None),
            P("pipe", "expert", None),
            P("pipe", None, "expert"),
            P("pipe", None),
            P("pipe", None),
        ),
        check_vma=False,
    )
```

```python
import math

import jax
import jax.numpy as jnp
from jax import lax
from jax.experimental import pallas as pl
from jax.experimental.pallas import tpu as pltpu
from jax.sharding import PartitionSpec as P

D = 7168
HID = 1024
EXPERTS = 4
PARTS = 8
PEERS = EXPERTS * PARTS
TOK = 64
MAIN = 32
TILE = 16
WIDTH = D // PARTS
BLOCKS = WIDTH // 128
ROWS_MAIN = PEERS * MAIN
ROWS_LEFT = PEERS * 2
ROWS = ROWS_MAIN + ROWS_LEFT
FOLDED = PEERS * TILE
N_PIPE = 8

qlimit = 7.0
epsilon = 1e-06
MESH = pl.DeviceIdType.MESH
F32 = jnp.float32
BF16 = jnp.bfloat16

SIN_PI = (3.1415927410125732, -5.167710304260254, 2.550077438354492, -0.598291277885437, 0.07765766233205795)
COS_PI = (
    1.0,
    -4.934802055358887,
    4.058709144592285,
    -1.335211992263794,
    0.23493731021881104,
    -0.024396324530243874,
)
NN = (((1,), (0,)), ((), ()))
NT = (((1,), (1,)), ((), ()))
TN = (((0,), (0,)), ((), ()))
U, C, A = 0, 1, 2


def dot(a, b, dims=NN):
    return lax.dot_general(a, b, dims, preferred_element_type=F32)


def poly(coefs, square):
    total = coefs[-1]
    for coef in coefs[-2::-1]:
        total = total * square + coef
    return total


def waves(weights, inverse):
    ratio = weights.astype(F32) * inverse
    clipped = jnp.clip(ratio, -qlimit, qlimit)
    rest = clipped - jnp.round(clipped)
    square = rest * rest
    sine = rest * poly(SIN_PI, square)
    return clipped, jnp.abs(ratio) < qlimit, sine, sine * poly(COS_PI, square) * (1.0 / math.pi)


def iota(shape, axis):
    return lax.broadcasted_iota(jnp.int32, shape, axis)


def at(index, size):
    return pl.ds(pl.multiple_of(index * size, size), size)


def pack_tables(routes, gates):
    members = jnp.concatenate(
        [((routes[0:1] == e) | (routes[1:2] == e)).astype(F32) for e in range(EXPERTS)]
        + [jnp.zeros((EXPERTS, TOK), F32)],
        axis=0,
    )
    earlier = (iota((TOK, TOK), 0) < iota((TOK, TOK), 1)).astype(F32)
    slots = dot(members.astype(BF16), earlier.astype(BF16))
    main, left, main_gate, left_gate = [], [], [], []
    for e in range(EXPERTS):
        gate = jnp.where(routes[0:1] == e, gates[0:1], 0.0) + jnp.where(
            routes[1:2] == e, gates[1:2], 0.0
        )
        named = members[e : e + 1] > 0.5
        slot = slots[e : e + 1].astype(jnp.int32)
        for rows, tables, gated in ((MAIN, main, main_gate), (TILE, left, left_gate)):
            place = iota((rows, TOK), 0)
            if rows == TILE:
                place = MAIN + lax.rem(place, 2)
            table = ((place == slot) & named).astype(F32)
            tables.append(table)
            gated.append(jnp.sum(table * gate, axis=1, keepdims=True))
    table = jnp.concatenate(main + left, axis=0).astype(BF16)
    return table, jnp.concatenate(main_gate + left_gate, axis=0)


def unpack_tables(routes, gates):
    lane = iota((TOK, 128), 1).astype(F32)
    members = ((lane == routes[:, 0:1]) | (lane == routes[:, 1:2])).astype(F32)
    earlier = (iota((TOK, TOK), 0) > iota((TOK, TOK), 1)).astype(F32)
    slots = dot(earlier.astype(BF16), members.astype(BF16)).astype(jnp.int32)
    main = jnp.zeros((TOK, EXPERTS * MAIN), F32)
    folded = jnp.zeros((TOK, EXPERTS * TILE), F32)
    lane_main = iota(main.shape, 1)
    lane_fold = iota(folded.shape, 1)
    for e in range(EXPERTS):
        if gates is None:
            value = members[:, e : e + 1]
        else:
            value = jnp.where(routes[:, 0:1] == e, gates[:, 0:1], 0.0) + jnp.where(
                routes[:, 1:2] == e, gates[:, 1:2], 0.0
            )
        slot = slots[:, e : e + 1]
        main = main + jnp.where(lane_main == e * MAIN + slot, jnp.where(slot < MAIN, value, 0.0), 0.0)
        here = (lax.div(lane_fold, TILE) == e) & (MAIN + lax.rem(lane_fold, 2) == slot)
        folded = folded + jnp.where(here, value, 0.0)
    block = lax.div(lax.rem(lane_fold, TILE), 2)
    folded = jnp.concatenate([jnp.where(block == b, folded, 0.0) for b in range(BLOCKS)], axis=0)
    return main, folded


def terms(table, count):
    out = []
    for _ in range(count):
        out.append(table.astype(BF16))
        table = table - out[-1].astype(F32)
    return out


def kernel(
    xa, xb, cb, by_row, by_col, w_up, w_down, s_up, s_down,
    o_next, o_cot, o_up, o_down, o_sums,
    q_up, q_down, rows, folds, snd, snd_fold, ret, ret_fold,
    keep, send1, recv1, send2, recv2, send3, recv3, gathered,
    out_a, out_b, g_wide, unit_a, unit_b, sum_snd, sum_rcv,
    d_ss, d_rs, d_sf, d_rf, h_s, h_r, g_s, g_r, t_ss, t_rs, t_sf, t_rf, p_s, p_r, z_s, z_r,
):
    me = lax.axis_index("expert")
    pipe = lax.axis_index("pipe")
    mine = me // PARTS
    part = me % PARTS
    bits = (part % 2, (part // 2) % 2, part // 4)
    partners = [me + (1 << k) - (2 << k) * bits[k] for k in range(3)]

    barrier = pltpu.get_barrier_semaphore()

    @pl.loop(1, PEERS)
    def _(i):
        pl.semaphore_signal(barrier, inc=1, device_id=(pipe, (me + i) % PEERS), device_id_type=MESH)

    @pl.when(pipe > 0)
    def _():
        pl.semaphore_signal(barrier, inc=1, device_id=(pipe - 1, me), device_id_type=MESH)

    @pl.when(pipe < N_PIPE - 1)
    def _():
        pl.semaphore_signal(barrier, inc=1, device_id=(pipe + 1, me), device_id_type=MESH)

    def copy(src, dst, send_sem, recv_sem, to, along=None):
        return pltpu.make_async_remote_copy(
            src_ref=src,
            dst_ref=dst,
            send_sem=send_sem,
            recv_sem=recv_sem,
            device_id=(pipe if along is None else along, to),
            device_id_type=MESH,
        )

    def wait_for(ref, sem):
        pltpu.make_async_copy(ref, ref, sem).wait()

    def norm_of(x_ref, unit):
        def body(q, total):
            wide = x_ref[:, at(q, WIDTH)].astype(F32)
            return total + jnp.sum(wide * wide, axis=1, keepdims=True)

        total = lax.fori_loop(0, PARTS, body, jnp.zeros((TOK, 1), F32))
        unit[...] = jnp.broadcast_to(lax.rsqrt(total * (1.0 / D) + epsilon), unit.shape)

    fold_row = lax.div(lax.rem(iota((EXPERTS * TILE, 128), 0), TILE), 2)

    def dispatch(kind, slot, x_ref, table, unit, gate):
        def pack(q):
            values = x_ref[:, at(q, WIDTH)]
            if unit is not None:
                values = (values.astype(F32) * unit[:, 0:1]).astype(BF16)
            packed = dot(table, values)
            if gate is not None:
                packed = packed * gate
            left = jnp.zeros((EXPERTS * TILE, 128), F32)
            for b in range(BLOCKS):
                part_b = packed[EXPERTS * MAIN :, b * 128 : (b + 1) * 128]
                left = jnp.where(fold_row == b, part_b, left)
            for e in range(EXPERTS):
                to = e * PARTS + q
                snd[slot, at(to, MAIN), :] = packed[e * MAIN : (e + 1) * MAIN].astype(BF16)
                snd_fold[slot, at(to, TILE), :] = left[e * TILE : (e + 1) * TILE].astype(BF16)

        def send(to):
            copy(
                snd.at[slot, at(to, MAIN)], rows.at[kind, at(me, MAIN)], d_ss.at[slot], d_rs.at[kind], to
            ).start()
            copy(
                snd_fold.at[slot, at(to, TILE)], folds.at[kind, at(me, TILE)], d_sf.at[slot], d_rf.at[kind], to
            ).start()

        @pl.loop(1, PARTS)
        def _(s):
            q = (part + s) % PARTS
            pack(q)
            for r in range(EXPERTS):
                send(((mine + r) % EXPERTS) * PARTS + q)

        pack(part)
        for r in range(1, EXPERTS):
            send(((mine + r) % EXPERTS) * PARTS + part)
        rows[kind, at(me, MAIN), :] = snd[slot, at(me, MAIN), :]
        folds[kind, at(me, TILE), :] = snd_fold[slot, at(me, TILE), :]

    others_main = pl.ds(0, (PEERS - 1) * MAIN)
    others_fold = pl.ds(0, (PEERS - 1) * TILE)

    def sent(slot):
        wait_for(snd.at[slot, others_main], d_ss.at[slot])
        wait_for(snd_fold.at[slot, others_fold], d_sf.at[slot])

    def arrive(kind):
        wait_for(rows.at[kind, others_main], d_rs.at[kind])
        wait_for(folds.at[kind, others_fold], d_rf.at[kind])
        shape = (BLOCKS * ROWS_LEFT, FOLDED)
        to, come = iota(shape, 0), iota(shape, 1)
        place = lax.rem(to, ROWS_LEFT)
        wanted = lax.div(place, 2) * TILE + lax.div(to, ROWS_LEFT) * 2 + lax.rem(place, 2)
        spread = dot((come == wanted).astype(BF16), folds[kind])
        for b in range(BLOCKS):
            rows[kind, pl.ds(ROWS_MAIN, ROWS_LEFT), b * 128 : (b + 1) * 128] = spread[
                b * ROWS_LEFT : (b + 1) * ROWS_LEFT
            ].astype(BF16)

    def row_chunks(body):
        @pl.loop(0, 4)
        def _(i):
            body(at(i, 256), i)

        body(pl.ds(ROWS_MAIN, ROWS_LEFT), None)

    def step_1(kind, held):
        def body(chunk, _):
            lhs = rows[kind, chunk, :]
            for k in range(4):
                span = slice(k * 256, (k + 1) * 256)
                both = dot(lhs, q_down[span, :], NT) if kind == C else dot(lhs, q_up[:, span])
                low, high = both[:, :128], both[:, 128:]
                odd = bits[0] == 1
                keep[held, k, chunk, :] = jnp.where(odd, high, low)
                send1[kind, k, chunk, :] = jnp.where(odd, low, high).astype(BF16)

        row_chunks(body)
        copy(send1.at[kind], recv1.at[kind], h_s.at[0, kind], h_r.at[0, kind], partners[0]).start()

    def step_2(kind, held):
        wait_for(recv1.at[kind], h_r.at[0, kind])
        for m in range(2):
            give = 2 * m + 1 - bits[1]
            send2[kind, m] = (keep[held, give] + recv1[kind, give].astype(F32)).astype(BF16)
        copy(send2.at[kind], recv2.at[kind], h_s.at[1, kind], h_r.at[1, kind], partners[1]).start()
        for m in range(2):
            own = 2 * m + bits[1]
            keep[held, own] = keep[held, own] + recv1[kind, own].astype(F32)

    def step_3(kind, held):
        wait_for(recv2.at[kind], h_r.at[1, kind])
        give = 1 - bits[2]
        send3[kind] = (keep[held, 2 * give + bits[1]] + recv2[kind, give].astype(F32)).astype(BF16)
        copy(send3.at[kind], recv3.at[kind], h_s.at[2, kind], h_r.at[2, kind], partners[2]).start()

    def summed(kind, held, chunk):
        own = bits[2]
        total = keep[held, 2 * own + bits[1], chunk, :] + recv2[kind, own, chunk, :].astype(F32)
        return (total + recv3[kind, chunk, :].astype(F32)).astype(BF16).astype(F32)

    def gather(kind, step):
        if step == 0:
            blocks = [part]
        elif step == 1:
            blocks = [bits[0] + 2 * bits[1], bits[0] + 2 * bits[1] + 4]
        else:
            blocks = [2 * k + bits[0] for k in range(4)]
        for block in blocks:
            copy(
                gathered.at[kind, block], gathered.at[kind, block],
                g_s.at[step, kind], g_r.at[step, kind], partners[2 - step],
            ).start()

    def gather_wait(kind, step):
        wait_for(gathered.at[kind, pl.ds(0, 1 << step)], g_r.at[step, kind])

    def wide(kind, chunk):
        return jnp.concatenate([gathered[kind, j, chunk, :] for j in range(PARTS)], axis=1)

    def give_back(slot, made):
        @pl.loop(0, 4)
        def _(i):
            snd[slot, at(i, 256), :] = made(at(i, 256)).astype(BF16)

        left = made(pl.ds(ROWS_MAIN, ROWS_LEFT)).astype(BF16)
        shape = (FOLDED, BLOCKS * ROWS_LEFT)
        to, come = iota(shape, 0), iota(shape, 1)
        inner = lax.rem(to, TILE)
        wanted = lax.div(inner, 2) * ROWS_LEFT + lax.div(to, TILE) * 2 + lax.rem(inner, 2)
        stacked = jnp.concatenate([left[:, b * 128 : (b + 1) * 128] for b in range(BLOCKS)], axis=0)
        snd_fold[slot] = dot((come == wanted).astype(BF16), stacked).astype(BF16)

        def send(to):
            copy(
                snd.at[slot, at(to, MAIN)], ret.at[slot, at(me, MAIN)], t_ss.at[slot], t_rs.at[slot, part], to
            ).start()
            copy(
                snd_fold.at[slot, at(to, TILE)], ret_fold.at[slot, at(me, TILE)],
                t_sf.at[slot], t_rf.at[slot, part], to,
            ).start()

        @pl.loop(1, PEERS)
        def _(i):
            send((me + i) % PEERS)

        ret[slot, at(me, MAIN), :] = snd[slot, at(me, MAIN), :]
        ret_fold[slot, at(me, TILE), :] = snd_fold[slot, at(me, TILE), :]

    def come_back(slot, q, count):
        wait_for(ret.at[slot, pl.ds(0, count * MAIN)], t_rs.at[slot, q])
        wait_for(ret_fold.at[slot, pl.ds(0, count * TILE)], t_rf.at[slot, q])

    def combined(slot, q, mains, foldeds):
        come = jnp.concatenate([ret[slot, at(e * PARTS + q, MAIN), :] for e in range(EXPERTS)], axis=0)
        fold = jnp.concatenate([ret_fold[slot, at(e * PARTS + q, TILE), :] for e in range(EXPERTS)], axis=0)
        total = sum(dot(table, come) for table in mains)
        extra = sum(dot(table, fold) for table in foldeds)
        return total + jnp.concatenate([extra[b * TOK : (b + 1) * TOK] for b in range(BLOCKS)], axis=1)

    table_b, gate_b = pack_tables(by_row[4:6, :], by_row[6:8, :])
    norm_of(xb, unit_b)
    pl.semaphore_wait(
        barrier, PEERS - 1 + jnp.where(pipe > 0, 1, 0) + jnp.where(pipe < N_PIPE - 1, 1, 0)
    )
    dispatch(U, 0, xb, table_b, unit_b, None)
    dispatch(C, 1, cb, table_b, None, gate_b)

    step_up, step_down = s_up[0, mine], s_down[0, mine]
    one = jnp.ones((1, 1), F32)
    inv_up, inv_down = one / step_up, one / step_down

    @pl.loop(0, WIDTH // 64)
    def _(i):
        ratio, _, _, bend = waves(w_up[at(i, 64), :], inv_up)
        q_up[at(i, 64), :] = (step_up * (ratio - bend)).astype(BF16)

    @pl.loop(0, HID // 64)
    def _(i):
        ratio, _, _, bend = waves(w_down[at(i, 64), :], inv_down)
        q_down[at(i, 64), :] = (step_down * (ratio - bend)).astype(BF16)

    table_a, _ = pack_tables(by_row[0:2, :], by_row[2:4, :])
    norm_of(xa, unit_a)

    arrive(U)
    step_1(U, 0)
    sent(0)
    dispatch(A, 0, xa, table_a, unit_a, None)
    arrive(C)
    step_1(C, 1)
    step_2(U, 0)
    step_2(C, 1)
    step_3(U, 0)
    step_3(C, 1)
    wait_for(recv3.at[U], h_r.at[2, U])
    wait_for(recv3.at[C], h_r.at[2, C])

    def between(chunk, _):
        pre = summed(U, 0, chunk)
        grad = summed(C, 1, chunk)
        sigma = 1.0 / (1.0 + jnp.exp(-pre))
        gathered[U, part, chunk, :] = (grad * (sigma * (1.0 + pre * (1.0 - sigma)))).astype(BF16)
        gathered[C, part, chunk, :] = (pre * sigma).astype(BF16)

    row_chunks(between)
    gather(U, 0)
    gather(C, 0)
    arrive(A)
    step_1(A, 0)
    gather_wait(U, 0)
    gather(U, 1)
    gather_wait(C, 0)
    gather(C, 1)
    step_2(A, 0)
    gather_wait(U, 1)
    gather(U, 2)
    gather_wait(C, 1)
    gather(C, 2)
    step_3(A, 0)
    gather_wait(U, 2)
    sent(1)
    give_back(1, lambda chunk: dot(wide(U, chunk), q_up[...], NT))

    wait_for(recv3.at[A], h_r.at[2, A])

    def silu_rows(chunk, _):
        pre = summed(A, 0, chunk)
        gathered[A, part, chunk, :] = (pre / (1.0 + jnp.exp(-pre))).astype(BF16)

    row_chunks(silu_rows)
    gather(A, 0)
    gather_wait(A, 0)
    gather(A, 1)
    gather_wait(A, 1)
    gather(A, 2)
    gather_wait(C, 2)
    gather_wait(A, 2)
    sent(0)
    give_back(0, lambda chunk: dot(wide(A, chunk), q_down[...]))

    def quant_grads(weights, inverse, grads):
        ratio, inside, sine, bend = waves(weights, inverse)
        wave = jnp.where(inside, 2.0 * sine * sine, 0.0)
        grads = grads.astype(BF16).astype(F32)
        return (grads * wave).astype(BF16), jnp.sum(
            grads * (ratio - bend - ratio * wave), axis=0, keepdims=True
        )

    def up_body(i, total):
        lhs = rows[U, :, at(i, 128)]
        for k in range(4):
            rhs = jnp.concatenate([gathered[U, 2 * k], gathered[U, 2 * k + 1]], axis=1)
            span = slice(k * 256, (k + 1) * 256)
            out, partial = quant_grads(w_up[at(i, 128), span], inv_up, dot(lhs, rhs, TN))
            o_up[at(i, 128), span] = out
            total = total + partial
        return total

    def down_body(j, total):
        out, partial = quant_grads(w_down[at(j, 128), :], inv_down, dot(gathered[C, j], rows[C], TN))
        o_down[at(j, 128), :] = out
        return total + partial

    up_total = lax.fori_loop(0, BLOCKS, up_body, jnp.zeros((1, 256), F32))
    down_total = lax.fori_loop(0, PARTS, down_body, jnp.zeros((1, WIDTH), F32))
    first = iota((8, 128), 0) == 0
    scaled = 1.0 / math.sqrt(D * HID * qlimit)
    sum_snd[...] = (
        jnp.where(
            first,
            jnp.sum(up_total, axis=1, keepdims=True),
            jnp.sum(down_total, axis=1, keepdims=True),
        )
        * scaled
    )
    sum_rcv[me] = sum_snd[...]

    @pl.loop(1, PEERS)
    def _(i):
        copy(sum_snd, sum_rcv.at[me], z_s, z_r, (me + i) % PEERS).start()

    main_b, fold_b = unpack_tables(by_col[:, 4:6], None)
    main_b, fold_b = terms(main_b, 1), terms(fold_b, 1)

    def take_b(q):
        grads = combined(1, q, main_b, fold_b)
        g_wide[:, at(q, WIDTH)] = grads
        return jnp.sum(xb[:, at(q, WIDTH)].astype(F32) * grads, axis=1, keepdims=True)

    come_back(1, part, EXPERTS - 1)
    along = take_b(part)

    def body_b(s, total):
        q = (part + s) % PARTS
        come_back(1, q, EXPERTS)
        return total + take_b(q)

    along = lax.fori_loop(1, PARTS, body_b, along)
    unit = unit_b[:, 0:1]
    bent = along * unit * unit * unit * (1.0 / D)

    @pl.loop(0, PARTS)
    def _(q):
        span = at(q, WIDTH)
        back = g_wide[:, span] * unit - xb[:, span].astype(F32) * bent
        out_b[:, span] = (cb[:, span].astype(F32) + back).astype(BF16)

        @pl.when(pipe > 0)
        def _():
            copy(out_b.at[:, span], o_cot.at[:, span], p_s.at[1], p_r.at[1], me, pipe - 1).start()

    main_a, fold_a = unpack_tables(by_col[:, 0:2], by_col[:, 2:4])
    main_a, fold_a = terms(main_a, 3), terms(fold_a, 3)

    def take_a(q):
        span = at(q, WIDTH)
        out_a[:, span] = (xa[:, span].astype(F32) + combined(0, q, main_a, fold_a)).astype(BF16)

        @pl.when(pipe < N_PIPE - 1)
        def _():
            copy(out_a.at[:, span], o_next.at[:, span], p_s.at[0], p_r.at[0], me, pipe + 1).start()

    come_back(0, part, EXPERTS - 1)
    take_a(part)

    @pl.loop(1, PARTS)
    def _(s):
        q = (part + s) % PARTS
        come_back(0, q, EXPERTS)
        take_a(q)

    wait_for(sum_rcv.at[pl.ds(0, PEERS - 1)], z_r)
    for e in range(EXPERTS):
        o_sums[e] = sum(sum_rcv[e * PARTS + k] for k in range(PARTS))

    wait_for(sum_rcv.at[pl.ds(0, PEERS - 1)], z_s)
    for slot in (0, 1):
        wait_for(snd.at[slot, others_main], t_ss.at[slot])
        wait_for(snd_fold.at[slot, others_fold], t_sf.at[slot])
    for kind in (U, C, A):
        wait_for(send1.at[kind], h_s.at[0, kind])
        wait_for(send2.at[kind], h_s.at[1, kind])
        wait_for(send3.at[kind], h_s.at[2, kind])
        for step in range(3):
            wait_for(gathered.at[kind, pl.ds(0, 1 << step)], g_s.at[step, kind])

    @pl.when(pipe > 0)
    def _():
        wait_for(out_b, p_s.at[1])
        wait_for(o_next, p_r.at[0])

    @pl.when(pipe == 0)
    def _():
        o_next[...] = jnp.zeros_like(o_next)

    @pl.when(pipe < N_PIPE - 1)
    def _():
        wait_for(out_a, p_s.at[0])
        wait_for(o_cot, p_r.at[1])

    @pl.when(pipe == N_PIPE - 1)
    def _():
        o_cot[...] = jnp.zeros_like(o_cot)


def shards(
    acts_a, acts_b, cot_b, routes_a, gates_a, routes_b, gates_b, up_weight, down_weight, up_scale, down_scale
):
    by_col = jnp.concatenate(
        (routes_a[0].astype(F32), gates_a[0], routes_b[0].astype(F32), gates_b[0]), axis=1
    )
    vmem = pl.BlockSpec(memory_space=pltpu.VMEM)
    smem = pl.BlockSpec(memory_space=pltpu.SMEM)
    dma = pltpu.SemaphoreType.DMA

    def bf(*shape):
        return pltpu.VMEM(shape, BF16)

    def wide(*shape):
        return pltpu.VMEM(shape, F32)

    def out(*shape):
        return jax.ShapeDtypeStruct(shape, BF16)

    next_a, next_cot, dw_up, dw_down, sums = pl.pallas_call(
        kernel,
        out_shape=(
            out(TOK, D), out(TOK, D), out(WIDTH, HID), out(HID, WIDTH),
            jax.ShapeDtypeStruct((EXPERTS, 8, 128), F32),
        ),
        in_specs=[vmem] * 7 + [smem] * 2,
        out_specs=(vmem,) * 5,
        scratch_shapes=[
            bf(WIDTH, HID), bf(HID, WIDTH),
            bf(3, ROWS, WIDTH), bf(3, FOLDED, 128),
            bf(2, ROWS_MAIN, WIDTH), bf(2, FOLDED, 128),
            bf(2, ROWS_MAIN, WIDTH), bf(2, FOLDED, 128),
            wide(2, 4, ROWS, 128),
            bf(3, 4, ROWS, 128), bf(3, 4, ROWS, 128),
            bf(3, 2, ROWS, 128), bf(3, 2, ROWS, 128),
            bf(3, ROWS, 128), bf(3, ROWS, 128),
            bf(3, PARTS, ROWS, 128),
            bf(TOK, D), bf(TOK, D), wide(TOK, D),
            wide(TOK, 128), wide(TOK, 128),
            wide(8, 128), wide(PEERS, 8, 128),
            dma((2,)), dma((3,)), dma((2,)), dma((3,)),
            dma((3, 3)), dma((3, 3)), dma((3, 3)), dma((3, 3)),
            dma((2,)), dma((2, PARTS)), dma((2,)), dma((2, PARTS)),
            dma((2,)), dma((2,)), dma, dma,
        ],
        compiler_params=pltpu.CompilerParams(
            collective_id=0, has_side_effects=True, vmem_limit_bytes=62 << 20
        ),
    )(
        acts_a[0], acts_b[0], cot_b[0], by_col.T, by_col, up_weight[0], down_weight[0], up_scale, down_scale
    )
    return (
        next_a[None], next_cot[None], dw_up[None], dw_down[None], sums[None, :, 0, 0], sums[None, :, 1, 0],
    )


def solution(mesh):
    split, rows = P("pipe", "expert", None), P("pipe", None)
    columns = P("pipe", None, "expert")
    return jax.shard_map(
        shards,
        mesh=mesh,
        in_specs=(split,) * 8 + (columns, rows, rows),
        out_specs=(split, split, split, columns, rows, rows),
        check_vma=False,
    )
```

```python
import math

import jax
import jax.numpy as jnp
from jax import lax
from jax.experimental import pallas as pl
from jax.experimental.pallas import tpu as pltpu
from jax.sharding import PartitionSpec as P

D = 7168
HID = 1024
EXPERTS = 4
PARTS = 8
PEERS = EXPERTS * PARTS
TOK = 64
MAIN = 32
TILE = 16
WIDTH = D // PARTS
BLOCKS = WIDTH // 128
ROWS_MAIN = PEERS * MAIN
ROWS_LEFT = PEERS * 2
ROWS = ROWS_MAIN + ROWS_LEFT
FOLDED = PEERS * TILE
N_PIPE = 8
PIECES = 4

qlimit = 7.0
epsilon = 1e-06
MESH = pl.DeviceIdType.MESH
F32 = jnp.float32
BF16 = jnp.bfloat16

SIN_PI = (3.1415927410125732, -5.167710304260254, 2.550077438354492, -0.598291277885437, 0.07765766233205795)
COS_PI = (
    1.0,
    -4.934802055358887,
    4.058709144592285,
    -1.335211992263794,
    0.23493731021881104,
    -0.024396324530243874,
)
NN = (((1,), (0,)), ((), ()))
NT = (((1,), (1,)), ((), ()))
TN = (((0,), (0,)), ((), ()))
U, C, A = 0, 1, 2


def dot(a, b, dims=NN):
    return lax.dot_general(a, b, dims, preferred_element_type=F32)


def poly(coefs, square):
    total = coefs[-1]
    for coef in coefs[-2::-1]:
        total = total * square + coef
    return total


def waves(weights, inverse):
    ratio = weights.astype(F32) * inverse
    clipped = jnp.clip(ratio, -qlimit, qlimit)
    rest = clipped - jnp.round(clipped)
    square = rest * rest
    sine = rest * poly(SIN_PI, square)
    return clipped, jnp.abs(ratio) < qlimit, sine, sine * poly(COS_PI, square) * (1.0 / math.pi)


def iota(shape, axis):
    return lax.broadcasted_iota(jnp.int32, shape, axis)


def at(index, size):
    return pl.ds(pl.multiple_of(index * size, size), size)


def pack_tables(routes, gates):
    members = jnp.concatenate(
        [((routes[0:1] == e) | (routes[1:2] == e)).astype(F32) for e in range(EXPERTS)]
        + [jnp.zeros((EXPERTS, TOK), F32)],
        axis=0,
    )
    earlier = (iota((TOK, TOK), 0) < iota((TOK, TOK), 1)).astype(F32)
    slots = dot(members.astype(BF16), earlier.astype(BF16))
    main, left, main_gate, left_gate = [], [], [], []
    for e in range(EXPERTS):
        gate = jnp.where(routes[0:1] == e, gates[0:1], 0.0) + jnp.where(
            routes[1:2] == e, gates[1:2], 0.0
        )
        named = members[e : e + 1] > 0.5
        slot = slots[e : e + 1].astype(jnp.int32)
        for rows, tables, gated in ((MAIN, main, main_gate), (TILE, left, left_gate)):
            place = iota((rows, TOK), 0)
            if rows == TILE:
                place = MAIN + lax.rem(place, 2)
            table = ((place == slot) & named).astype(F32)
            tables.append(table)
            gated.append(jnp.sum(table * gate, axis=1, keepdims=True))
    table = jnp.concatenate(main + left, axis=0).astype(BF16)
    return table, jnp.concatenate(main_gate + left_gate, axis=0)


def unpack_tables(routes, gates):
    lane = iota((TOK, 128), 1).astype(F32)
    members = ((lane == routes[:, 0:1]) | (lane == routes[:, 1:2])).astype(F32)
    earlier = (iota((TOK, TOK), 0) > iota((TOK, TOK), 1)).astype(F32)
    slots = dot(earlier.astype(BF16), members.astype(BF16)).astype(jnp.int32)
    main = jnp.zeros((TOK, EXPERTS * MAIN), F32)
    folded = jnp.zeros((TOK, EXPERTS * TILE), F32)
    lane_main = iota(main.shape, 1)
    lane_fold = iota(folded.shape, 1)
    for e in range(EXPERTS):
        if gates is None:
            value = members[:, e : e + 1]
        else:
            value = jnp.where(routes[:, 0:1] == e, gates[:, 0:1], 0.0) + jnp.where(
                routes[:, 1:2] == e, gates[:, 1:2], 0.0
            )
        slot = slots[:, e : e + 1]
        main = main + jnp.where(lane_main == e * MAIN + slot, jnp.where(slot < MAIN, value, 0.0), 0.0)
        here = (lax.div(lane_fold, TILE) == e) & (MAIN + lax.rem(lane_fold, 2) == slot)
        folded = folded + jnp.where(here, value, 0.0)
    block = lax.div(lax.rem(lane_fold, TILE), 2)
    folded = jnp.concatenate([jnp.where(block == b, folded, 0.0) for b in range(BLOCKS)], axis=0)
    return main, folded


def terms(table, count):
    out = []
    for _ in range(count):
        out.append(table.astype(BF16))
        table = table - out[-1].astype(F32)
    return out


def kernel(
    xa, xb, cb, by_row, by_col, w_up, w_down, s_up, s_down,
    o_next, o_cot, o_up, o_down, o_sums,
    q_up, q_down, rows, folds, snd, snd_fold, ret, ret_fold,
    keep, send1, recv1, passed, gathered,
    out_a, out_b, g_wide, unit_a, unit_b, sum_snd, sum_rcv,
    d_ss, d_rs, d_sf, d_rf, h_s, h_r, l_s, l_r, g_s, g_r, c_s, c_r, t_ss, t_rs, t_sf, t_rf, p_s, p_r, z_s, z_r,
):
    me = lax.axis_index("expert")
    pipe = lax.axis_index("pipe")
    mine = me // PARTS
    part = me % PARTS
    core, chip = part % 2, part // 2
    other_core = me + 1 - 2 * core
    upper = chip // 2
    is_end = (chip % 3) == 0
    over, away = me + 2 - 4 * upper, me - 2 + 4 * upper

    barrier = pltpu.get_barrier_semaphore()

    @pl.loop(1, PEERS)
    def _(i):
        pl.semaphore_signal(barrier, inc=1, device_id=(pipe, (me + i) % PEERS), device_id_type=MESH)

    @pl.when(pipe > 0)
    def _():
        pl.semaphore_signal(barrier, inc=1, device_id=(pipe - 1, me), device_id_type=MESH)

    @pl.when(pipe < N_PIPE - 1)
    def _():
        pl.semaphore_signal(barrier, inc=1, device_id=(pipe + 1, me), device_id_type=MESH)

    def copy(src, dst, send_sem, recv_sem, to, along=None):
        return pltpu.make_async_remote_copy(
            src_ref=src,
            dst_ref=dst,
            send_sem=send_sem,
            recv_sem=recv_sem,
            device_id=(pipe if along is None else along, to),
            device_id_type=MESH,
        )

    def wait_for(ref, sem):
        pltpu.make_async_copy(ref, ref, sem).wait()

    def norm_of(x_ref, unit):
        def body(q, total):
            wide = x_ref[:, at(q, WIDTH)].astype(F32)
            return total + jnp.sum(wide * wide, axis=1, keepdims=True)

        total = lax.fori_loop(0, PARTS, body, jnp.zeros((TOK, 1), F32))
        unit[...] = jnp.broadcast_to(lax.rsqrt(total * (1.0 / D) + epsilon), unit.shape)

    fold_row = lax.div(lax.rem(iota((EXPERTS * TILE, 128), 0), TILE), 2)

    def dispatch(kind, slot, x_ref, table, unit, gate):
        def pack(q):
            values = x_ref[:, at(q, WIDTH)]
            if unit is not None:
                values = (values.astype(F32) * unit[:, 0:1]).astype(BF16)
            packed = dot(table, values)
            if gate is not None:
                packed = packed * gate
            left = jnp.zeros((EXPERTS * TILE, 128), F32)
            for b in range(BLOCKS):
                part_b = packed[EXPERTS * MAIN :, b * 128 : (b + 1) * 128]
                left = jnp.where(fold_row == b, part_b, left)
            for e in range(EXPERTS):
                to = e * PARTS + q
                snd[slot, at(to, MAIN), :] = packed[e * MAIN : (e + 1) * MAIN].astype(BF16)
                snd_fold[slot, at(to, TILE), :] = left[e * TILE : (e + 1) * TILE].astype(BF16)

        def send(to):
            copy(
                snd.at[slot, at(to, MAIN)], rows.at[kind, at(me, MAIN)], d_ss.at[slot], d_rs.at[kind], to
            ).start()
            copy(
                snd_fold.at[slot, at(to, TILE)], folds.at[kind, at(me, TILE)], d_sf.at[slot], d_rf.at[kind], to
            ).start()

        @pl.loop(1, PARTS)
        def _(s):
            q = (part + s) % PARTS
            pack(q)
            for r in range(EXPERTS):
                send(((mine + r) % EXPERTS) * PARTS + q)

        pack(part)
        for r in range(1, EXPERTS):
            send(((mine + r) % EXPERTS) * PARTS + part)
        rows[kind, at(me, MAIN), :] = snd[slot, at(me, MAIN), :]
        folds[kind, at(me, TILE), :] = snd_fold[slot, at(me, TILE), :]

    others_main = pl.ds(0, (PEERS - 1) * MAIN)
    others_fold = pl.ds(0, (PEERS - 1) * TILE)

    def sent(slot):
        wait_for(snd.at[slot, others_main], d_ss.at[slot])
        wait_for(snd_fold.at[slot, others_fold], d_sf.at[slot])

    def arrive(kind):
        wait_for(rows.at[kind, others_main], d_rs.at[kind])
        wait_for(folds.at[kind, others_fold], d_rf.at[kind])
        shape = (BLOCKS * ROWS_LEFT, FOLDED)
        to, come = iota(shape, 0), iota(shape, 1)
        place = lax.rem(to, ROWS_LEFT)
        wanted = lax.div(place, 2) * TILE + lax.div(to, ROWS_LEFT) * 2 + lax.rem(place, 2)
        spread = dot((come == wanted).astype(BF16), folds[kind])
        for b in range(BLOCKS):
            rows[kind, pl.ds(ROWS_MAIN, ROWS_LEFT), b * 128 : (b + 1) * 128] = spread[
                b * ROWS_LEFT : (b + 1) * ROWS_LEFT
            ].astype(BF16)

    def row_chunks(body):
        @pl.loop(0, 4)
        def _(i):
            body(at(i, 256), i)

        body(pl.ds(ROWS_MAIN, ROWS_LEFT), None)

    def step_1(kind, held):
        def body(chunk, _):
            lhs = rows[kind, chunk, :]
            for k in range(4):
                span = slice(k * 256, (k + 1) * 256)
                both = dot(lhs, q_down[span, :], NT) if kind == C else dot(lhs, q_up[:, span])
                low, high = both[:, :128], both[:, 128:]
                odd = core == 1
                keep[held, k, chunk, :] = jnp.where(odd, high, low)
                send1[kind, k, chunk, :] = jnp.where(odd, low, high).astype(BF16)

        row_chunks(body)
        copy(send1.at[kind], recv1.at[kind], h_s.at[kind], h_r.at[kind], other_core).start()

    def add_core(kind, held):
        wait_for(recv1.at[kind], h_r.at[kind])
        wait_for(send1.at[kind], h_s.at[kind])

        @pl.loop(0, 4)
        def _(k):
            keep[held, k] = keep[held, k] + recv1[kind, k].astype(F32)

    def half(kind, held, k, rows_at, to, step, come):
        total = keep[held, k, rows_at, :]
        if come:
            wait_for(passed.at[kind, k, rows_at], l_r.at[kind, k, step])
            total = total + passed[kind, k, rows_at, :].astype(F32)
        send1[kind, k, rows_at, :] = total.astype(BF16)
        copy(
            send1.at[kind, k, rows_at], passed.at[kind, k, rows_at], l_s.at[kind], l_r.at[kind, k, step], to
        ).start()

    def piece(n):
        return pl.ds(n % 2 * (ROWS // 2), ROWS // 2)

    def line_ends(kind, held):
        @pl.when(is_end)
        def _():
            for n in range(PIECES):
                half(kind, held, 2 - 2 * upper + n // 2, piece(n), over, n % 2, False)

    def line_mids(kind, held, n):
        @pl.when(jnp.logical_not(is_end))
        def _():
            if n < PIECES:
                half(kind, held, 2 - 2 * upper + n // 2, piece(n), over, n % 2, True)
            if n > 0:
                half(kind, held, 2 * upper + (n - 1) // 2, piece(n - 1), away, (n - 1) % 2, True)

    def line_come(kind, k, n):
        wait_for(passed.at[kind, k, piece(n)], l_r.at[kind, k, n % 2])

    def summed(kind, held, k, chunk):
        total = keep[held, k, chunk, :] + passed[kind, k, chunk, :].astype(F32)
        return total.astype(BF16).astype(F32)

    def hand(kind, k, n, to):
        span = gathered.at[kind, 2 * k + core, piece(n)]
        copy(span, span, g_s.at[kind], g_r.at[kind, k, n % 2], to).start()

    def hand_core(kind, k, n):
        span = gathered.at[kind, 2 * k + core, piece(n)]
        copy(span, span, c_s.at[kind], c_r.at[kind], other_core).start()

    def gather_own(kind, n):
        k = 2 * upper + n // 2
        hand(kind, k, n, over)
        hand_core(kind, k, n)

    def gather_mids(kind, n):
        @pl.when(jnp.logical_not(is_end))
        def _():
            for p, to in ((n, over), (n - 1, away)):
                if 0 <= p < PIECES:
                    k = (2 * upper if p == n else 2 - 2 * upper) + p // 2
                    wait_for(gathered.at[kind, 0, piece(p)], g_r.at[kind, k, p % 2])
                    hand(kind, k, p, to)
                    hand_core(kind, k, p)

    def gather_ends(kind):
        @pl.when(is_end)
        def _():
            for n in range(PIECES):
                k = 2 - 2 * upper + n // 2
                wait_for(gathered.at[kind, 0, piece(n)], g_r.at[kind, k, n % 2])
                hand_core(kind, k, n)

        wait_for(gathered.at[kind, pl.ds(0, 4)], c_r.at[kind])

    def wide(kind, chunk):
        return jnp.concatenate([gathered[kind, j, chunk, :] for j in range(PARTS)], axis=1)

    def give_back(slot, made):
        @pl.loop(0, 4)
        def _(i):
            snd[slot, at(i, 256), :] = made(at(i, 256)).astype(BF16)

        left = made(pl.ds(ROWS_MAIN, ROWS_LEFT)).astype(BF16)
        shape = (FOLDED, BLOCKS * ROWS_LEFT)
        to, come = iota(shape, 0), iota(shape, 1)
        inner = lax.rem(to, TILE)
        wanted = lax.div(inner, 2) * ROWS_LEFT + lax.div(to, TILE) * 2 + lax.rem(inner, 2)
        stacked = jnp.concatenate([left[:, b * 128 : (b + 1) * 128] for b in range(BLOCKS)], axis=0)
        snd_fold[slot] = dot((come == wanted).astype(BF16), stacked).astype(BF16)

        def send(to):
            copy(
                snd.at[slot, at(to, MAIN)], ret.at[slot, at(me, MAIN)], t_ss.at[slot], t_rs.at[slot, part], to
            ).start()
            copy(
                snd_fold.at[slot, at(to, TILE)], ret_fold.at[slot, at(me, TILE)],
                t_sf.at[slot], t_rf.at[slot, part], to,
            ).start()

        @pl.loop(1, PARTS)
        def _(s):
            for r in range(EXPERTS):
                send(((mine + r) % EXPERTS) * PARTS + (part + s) % PARTS)

        for r in range(1, EXPERTS):
            send(((mine + r) % EXPERTS) * PARTS + part)
        ret[slot, at(me, MAIN), :] = snd[slot, at(me, MAIN), :]
        ret_fold[slot, at(me, TILE), :] = snd_fold[slot, at(me, TILE), :]

    def come_back(slot, q, count):
        wait_for(ret.at[slot, pl.ds(0, count * MAIN)], t_rs.at[slot, q])
        wait_for(ret_fold.at[slot, pl.ds(0, count * TILE)], t_rf.at[slot, q])

    def combined(slot, q, mains, foldeds):
        come = jnp.concatenate([ret[slot, at(e * PARTS + q, MAIN), :] for e in range(EXPERTS)], axis=0)
        fold = jnp.concatenate([ret_fold[slot, at(e * PARTS + q, TILE), :] for e in range(EXPERTS)], axis=0)
        total = sum(dot(table, come) for table in mains)
        extra = sum(dot(table, fold) for table in foldeds)
        return total + jnp.concatenate([extra[b * TOK : (b + 1) * TOK] for b in range(BLOCKS)], axis=1)

    table_b, gate_b = pack_tables(by_row[4:6, :], by_row[6:8, :])
    norm_of(xb, unit_b)
    pl.semaphore_wait(
        barrier, PEERS - 1 + jnp.where(pipe > 0, 1, 0) + jnp.where(pipe < N_PIPE - 1, 1, 0)
    )
    dispatch(U, 0, xb, table_b, unit_b, None)
    dispatch(C, 1, cb, table_b, None, gate_b)

    step_up, step_down = s_up[0, mine], s_down[0, mine]
    one = jnp.ones((1, 1), F32)
    inv_up, inv_down = one / step_up, one / step_down

    @pl.loop(0, WIDTH // 64)
    def _(i):
        ratio, _, _, bend = waves(w_up[at(i, 64), :], inv_up)
        q_up[at(i, 64), :] = (step_up * (ratio - bend)).astype(BF16)

    @pl.loop(0, HID // 64)
    def _(i):
        ratio, _, _, bend = waves(w_down[at(i, 64), :], inv_down)
        q_down[at(i, 64), :] = (step_down * (ratio - bend)).astype(BF16)

    table_a, _ = pack_tables(by_row[0:2, :], by_row[2:4, :])
    norm_of(xa, unit_a)

    arrive(U)
    step_1(U, 0)
    sent(0)
    dispatch(A, 0, xa, table_a, unit_a, None)
    arrive(C)
    step_1(C, 1)
    add_core(U, 0)
    line_ends(U, 0)
    add_core(C, 1)
    line_ends(C, 1)
    for n in range(PIECES + 1):
        line_mids(U, 0, n)
        line_mids(C, 1, n)

    @pl.when(is_end)
    def _():
        for n in range(PIECES):
            k = 2 * upper + n // 2
            chunk = piece(n)
            line_come(U, k, n)
            line_come(C, k, n)
            pre = summed(U, 0, k, chunk)
            grad = summed(C, 1, k, chunk)
            sigma = 1.0 / (1.0 + jnp.exp(-pre))
            gathered[U, 2 * k + core, chunk, :] = (grad * (sigma * (1.0 + pre * (1.0 - sigma)))).astype(BF16)
            gathered[C, 2 * k + core, chunk, :] = (pre * sigma).astype(BF16)
            gather_own(U, n)
            gather_own(C, n)

    arrive(A)
    step_1(A, 0)
    for n in range(2):
        gather_mids(U, n)
        gather_mids(C, n)
    add_core(A, 0)
    line_ends(A, 0)
    for n in range(2, PIECES + 1):
        gather_mids(U, n)
        gather_mids(C, n)
    for n in range(PIECES + 1):
        line_mids(A, 0, n)
    gather_ends(U)
    sent(1)
    give_back(1, lambda chunk: dot(wide(U, chunk), q_up[...], NT))

    @pl.when(is_end)
    def _():
        for n in range(PIECES):
            k = 2 * upper + n // 2
            chunk = piece(n)
            line_come(A, k, n)
            pre = summed(A, 0, k, chunk)
            gathered[A, 2 * k + core, chunk, :] = (pre / (1.0 + jnp.exp(-pre))).astype(BF16)
            gather_own(A, n)

    for n in range(PIECES + 1):
        gather_mids(A, n)
    gather_ends(C)
    gather_ends(A)
    sent(0)
    give_back(0, lambda chunk: dot(wide(A, chunk), q_down[...]))

    main_b, fold_b = unpack_tables(by_col[:, 4:6], None)
    main_b, fold_b = terms(main_b, 1), terms(fold_b, 1)

    def take_b(q):
        grads = combined(1, q, main_b, fold_b)
        g_wide[:, at(q, WIDTH)] = grads
        return jnp.sum(xb[:, at(q, WIDTH)].astype(F32) * grads, axis=1, keepdims=True)

    def body_b(s, total):
        q = (part + PARTS - s) % PARTS
        come_back(1, q, EXPERTS)
        return total + take_b(q)

    along = lax.fori_loop(1, PARTS, body_b, jnp.zeros((TOK, 1), F32))
    come_back(1, part, EXPERTS - 1)
    along = along + take_b(part)
    unit = unit_b[:, 0:1]
    bent = along * unit * unit * unit * (1.0 / D)

    @pl.loop(0, PARTS)
    def _(q):
        span = at(q, WIDTH)
        back = g_wide[:, span] * unit - xb[:, span].astype(F32) * bent
        out_b[:, span] = (cb[:, span].astype(F32) + back).astype(BF16)

        @pl.when(pipe > 0)
        def _():
            copy(out_b.at[:, span], o_cot.at[:, span], p_s.at[1], p_r.at[1], me, pipe - 1).start()

    def quant_grads(weights, inverse, grads):
        ratio, inside, sine, bend = waves(weights, inverse)
        wave = jnp.where(inside, 2.0 * sine * sine, 0.0)
        grads = grads.astype(BF16).astype(F32)
        return (grads * wave).astype(BF16), jnp.sum(
            grads * (ratio - bend - ratio * wave), axis=0, keepdims=True
        )

    def up_body(i, total):
        lhs = rows[U, :, at(i, 128)]
        for k in range(4):
            rhs = jnp.concatenate([gathered[U, 2 * k], gathered[U, 2 * k + 1]], axis=1)
            span = slice(k * 256, (k + 1) * 256)
            out, partial = quant_grads(w_up[at(i, 128), span], inv_up, dot(lhs, rhs, TN))
            o_up[at(i, 128), span] = out
            total = total + partial
        return total

    def down_body(j, total):
        out, partial = quant_grads(w_down[at(j, 128), :], inv_down, dot(gathered[C, j], rows[C], TN))
        o_down[at(j, 128), :] = out
        return total + partial

    up_total = lax.fori_loop(0, BLOCKS, up_body, jnp.zeros((1, 256), F32))
    down_total = lax.fori_loop(0, PARTS, down_body, jnp.zeros((1, WIDTH), F32))
    first = iota((8, 128), 0) == 0
    scaled = 1.0 / math.sqrt(D * HID * qlimit)
    sum_snd[...] = (
        jnp.where(
            first,
            jnp.sum(up_total, axis=1, keepdims=True),
            jnp.sum(down_total, axis=1, keepdims=True),
        )
        * scaled
    )
    sum_rcv[me] = sum_snd[...]

    @pl.loop(1, PEERS)
    def _(i):
        copy(sum_snd, sum_rcv.at[me], z_s, z_r, (me + i) % PEERS).start()

    main_a, fold_a = unpack_tables(by_col[:, 0:2], by_col[:, 2:4])
    main_a, fold_a = terms(main_a, 3), terms(fold_a, 3)

    def take_a(q):
        span = at(q, WIDTH)
        out_a[:, span] = (xa[:, span].astype(F32) + combined(0, q, main_a, fold_a)).astype(BF16)

        @pl.when(pipe < N_PIPE - 1)
        def _():
            copy(out_a.at[:, span], o_next.at[:, span], p_s.at[0], p_r.at[0], me, pipe + 1).start()

    @pl.loop(1, PARTS)
    def _(s):
        q = (part + PARTS - s) % PARTS
        come_back(0, q, EXPERTS)
        take_a(q)

    come_back(0, part, EXPERTS - 1)
    take_a(part)

    wait_for(sum_rcv.at[pl.ds(0, PEERS - 1)], z_r)
    for e in range(EXPERTS):
        o_sums[e] = sum(sum_rcv[e * PARTS + k] for k in range(PARTS))

    wait_for(sum_rcv.at[pl.ds(0, PEERS - 1)], z_s)
    for slot in (0, 1):
        wait_for(snd.at[slot, others_main], t_ss.at[slot])
        wait_for(snd_fold.at[slot, others_fold], t_sf.at[slot])
    for kind in (U, C, A):
        wait_for(gathered.at[kind, pl.ds(0, 4)], c_s.at[kind])

        @pl.when(is_end)
        def _():
            wait_for(send1.at[kind, pl.ds(0, 2)], l_s.at[kind])
            wait_for(gathered.at[kind, pl.ds(0, 2)], g_s.at[kind])

        @pl.when(jnp.logical_not(is_end))
        def _():
            wait_for(send1.at[kind], l_s.at[kind])
            wait_for(gathered.at[kind, pl.ds(0, 4)], g_s.at[kind])

    @pl.when(pipe > 0)
    def _():
        wait_for(out_b, p_s.at[1])
        wait_for(o_next, p_r.at[0])

    @pl.when(pipe == 0)
    def _():
        o_next[...] = jnp.zeros_like(o_next)

    @pl.when(pipe < N_PIPE - 1)
    def _():
        wait_for(out_a, p_s.at[0])
        wait_for(o_cot, p_r.at[1])

    @pl.when(pipe == N_PIPE - 1)
    def _():
        o_cot[...] = jnp.zeros_like(o_cot)


def shards(
    acts_a, acts_b, cot_b, routes_a, gates_a, routes_b, gates_b, up_weight, down_weight, up_scale, down_scale
):
    by_col = jnp.concatenate(
        (routes_a[0].astype(F32), gates_a[0], routes_b[0].astype(F32), gates_b[0]), axis=1
    )
    vmem = pl.BlockSpec(memory_space=pltpu.VMEM)
    smem = pl.BlockSpec(memory_space=pltpu.SMEM)
    dma = pltpu.SemaphoreType.DMA

    def bf(*shape):
        return pltpu.VMEM(shape, BF16)

    def wide(*shape):
        return pltpu.VMEM(shape, F32)

    def out(*shape):
        return jax.ShapeDtypeStruct(shape, BF16)

    next_a, next_cot, dw_up, dw_down, sums = pl.pallas_call(
        kernel,
        out_shape=(
            out(TOK, D), out(TOK, D), out(WIDTH, HID), out(HID, WIDTH),
            jax.ShapeDtypeStruct((EXPERTS, 8, 128), F32),
        ),
        in_specs=[vmem] * 7 + [smem] * 2,
        out_specs=(vmem,) * 5,
        scratch_shapes=[
            bf(WIDTH, HID), bf(HID, WIDTH),
            bf(3, ROWS, WIDTH), bf(3, FOLDED, 128),
            bf(2, ROWS_MAIN, WIDTH), bf(2, FOLDED, 128),
            bf(2, ROWS_MAIN, WIDTH), bf(2, FOLDED, 128),
            wide(2, 4, ROWS, 128),
            bf(3, 4, ROWS, 128), bf(3, 4, ROWS, 128),
            bf(3, 4, ROWS, 128),
            bf(3, PARTS, ROWS, 128),
            bf(TOK, D), bf(TOK, D), wide(TOK, D),
            wide(TOK, 128), wide(TOK, 128),
            wide(8, 128), wide(PEERS, 8, 128),
            dma((2,)), dma((3,)), dma((2,)), dma((3,)),
            dma((3,)), dma((3,)), dma((3,)), dma((3, 4, 2)), dma((3,)), dma((3, 4, 2)), dma((3,)), dma((3,)),
            dma((2,)), dma((2, PARTS)), dma((2,)), dma((2, PARTS)),
            dma((2,)), dma((2,)), dma, dma,
        ],
        compiler_params=pltpu.CompilerParams(
            collective_id=0, has_side_effects=True, vmem_limit_bytes=62 << 20
        ),
    )(
        acts_a[0], acts_b[0], cot_b[0], by_col.T, by_col, up_weight[0], down_weight[0], up_scale, down_scale
    )
    return (
        next_a[None], next_cot[None], dw_up[None], dw_down[None], sums[None, :, 0, 0], sums[None, :, 1, 0],
    )


def solution(mesh):
    split, rows = P("pipe", "expert", None), P("pipe", None)
    columns = P("pipe", None, "expert")
    return jax.shard_map(
        shards,
        mesh=mesh,
        in_specs=(split,) * 8 + (columns, rows, rows),
        out_specs=(split, split, split, columns, rows, rows),
        check_vma=False,
    )
```

```python
import math

import jax
import jax.numpy as jnp
from jax import lax
from jax.experimental import pallas as pl
from jax.experimental.pallas import tpu as pltpu
from jax.sharding import PartitionSpec as P

D = 7168
HID = 1024
EXPERTS = 4
PARTS = 8
PEERS = EXPERTS * PARTS
TOK = 64
MAIN = 32
TILE = 16
WIDTH = D // PARTS
BLOCKS = WIDTH // 128
ROWS_MAIN = PEERS * MAIN
ROWS_LEFT = PEERS * 2
ROWS = ROWS_MAIN + ROWS_LEFT
FOLDED = PEERS * TILE
N_PIPE = 8
PIECES = 4

qlimit = 7.0
epsilon = 1e-06
MESH = pl.DeviceIdType.MESH
F32 = jnp.float32
BF16 = jnp.bfloat16

SIN_PI = (3.1415927410125732, -5.167710304260254, 2.550077438354492, -0.598291277885437, 0.07765766233205795)
COS_PI = (
    1.0,
    -4.934802055358887,
    4.058709144592285,
    -1.335211992263794,
    0.23493731021881104,
    -0.024396324530243874,
)
NN = (((1,), (0,)), ((), ()))
NT = (((1,), (1,)), ((), ()))
TN = (((0,), (0,)), ((), ()))
U, C, A = 0, 1, 2


def dot(a, b, dims=NN):
    return lax.dot_general(a, b, dims, preferred_element_type=F32)


def poly(coefs, square):
    total = coefs[-1]
    for coef in coefs[-2::-1]:
        total = total * square + coef
    return total


def waves(weights, inverse):
    ratio = weights.astype(F32) * inverse
    clipped = jnp.clip(ratio, -qlimit, qlimit)
    rest = clipped - jnp.round(clipped)
    square = rest * rest
    sine = rest * poly(SIN_PI, square)
    return clipped, jnp.abs(ratio) < qlimit, sine, sine * poly(COS_PI, square) * (1.0 / math.pi)


def iota(shape, axis):
    return lax.broadcasted_iota(jnp.int32, shape, axis)


def at(index, size):
    return pl.ds(pl.multiple_of(index * size, size), size)


def pack_tables(routes, gates):
    members = jnp.concatenate(
        [((routes[0:1] == e) | (routes[1:2] == e)).astype(F32) for e in range(EXPERTS)]
        + [jnp.zeros((EXPERTS, TOK), F32)],
        axis=0,
    )
    earlier = (iota((TOK, TOK), 0) < iota((TOK, TOK), 1)).astype(F32)
    slots = dot(members.astype(BF16), earlier.astype(BF16))
    main, left, main_gate, left_gate = [], [], [], []
    for e in range(EXPERTS):
        gate = jnp.where(routes[0:1] == e, gates[0:1], 0.0) + jnp.where(
            routes[1:2] == e, gates[1:2], 0.0
        )
        named = members[e : e + 1] > 0.5
        slot = slots[e : e + 1].astype(jnp.int32)
        for rows, tables, gated in ((MAIN, main, main_gate), (TILE, left, left_gate)):
            place = iota((rows, TOK), 0)
            if rows == TILE:
                place = MAIN + lax.rem(place, 2)
            table = ((place == slot) & named).astype(F32)
            tables.append(table)
            gated.append(jnp.sum(table * gate, axis=1, keepdims=True))
    table = jnp.concatenate(main + left, axis=0).astype(BF16)
    return table, jnp.concatenate(main_gate + left_gate, axis=0)


def unpack_tables(routes, gates):
    lane = iota((TOK, 128), 1).astype(F32)
    members = ((lane == routes[:, 0:1]) | (lane == routes[:, 1:2])).astype(F32)
    earlier = (iota((TOK, TOK), 0) > iota((TOK, TOK), 1)).astype(F32)
    slots = dot(earlier.astype(BF16), members.astype(BF16)).astype(jnp.int32)
    main = jnp.zeros((TOK, EXPERTS * MAIN), F32)
    folded = jnp.zeros((TOK, EXPERTS * TILE), F32)
    lane_main = iota(main.shape, 1)
    lane_fold = iota(folded.shape, 1)
    for e in range(EXPERTS):
        if gates is None:
            value = members[:, e : e + 1]
        else:
            value = jnp.where(routes[:, 0:1] == e, gates[:, 0:1], 0.0) + jnp.where(
                routes[:, 1:2] == e, gates[:, 1:2], 0.0
            )
        slot = slots[:, e : e + 1]
        main = main + jnp.where(lane_main == e * MAIN + slot, jnp.where(slot < MAIN, value, 0.0), 0.0)
        here = (lax.div(lane_fold, TILE) == e) & (MAIN + lax.rem(lane_fold, 2) == slot)
        folded = folded + jnp.where(here, value, 0.0)
    block = lax.div(lax.rem(lane_fold, TILE), 2)
    folded = jnp.concatenate([jnp.where(block == b, folded, 0.0) for b in range(BLOCKS)], axis=0)
    return main, folded


def terms(table, count):
    out = []
    for _ in range(count):
        out.append(table.astype(BF16))
        table = table - out[-1].astype(F32)
    return out


def kernel(
    xa_from, xb, cb_from, routes_a, gates_a, routes_b, gates_b, w_up_from, w_down_from, s_up, s_down,
    o_next, o_cot, up_to, down_to, o_up_sums, o_down_sums,
    xa, cb, w_up, w_down, o_up, o_down, i_s, o_s,
    q_up, q_down, rows, folds, snd, snd_fold, ret, ret_fold,
    keep, send1, recv1, passed, gathered,
    out_a, out_b, g_wide, unit_a, unit_b, up_total, down_total, sum_snd, sum_rcv,
    d_ss, d_rs, d_sf, d_rf, h_s, h_r, l_s, l_r, g_s, g_r, c_s, c_r, t_ss, t_rs, t_sf, t_rf, p_s, p_r, z_s, z_r,
):
    me = lax.axis_index("expert")
    pipe = lax.axis_index("pipe")
    mine = me // PARTS
    part = me % PARTS
    core, chip = part % 2, part // 2
    other_core = me + 1 - 2 * core
    upper = chip // 2
    is_end = (chip % 3) == 0
    over, away = me + 2 - 4 * upper, me - 2 + 4 * upper

    loads = [
        pltpu.make_async_copy(src, dst, i_s.at[i])
        for i, (src, dst) in enumerate(
            ((cb_from, cb), (w_up_from, w_up), (w_down_from, w_down), (xa_from, xa))
        )
    ]
    for load in loads:
        load.start()

    barrier = pltpu.get_barrier_semaphore()

    @pl.loop(1, PEERS)
    def _(i):
        pl.semaphore_signal(barrier, inc=1, device_id=(pipe, (me + i) % PEERS), device_id_type=MESH)

    @pl.when(pipe > 0)
    def _():
        pl.semaphore_signal(barrier, inc=1, device_id=(pipe - 1, me), device_id_type=MESH)

    @pl.when(pipe < N_PIPE - 1)
    def _():
        pl.semaphore_signal(barrier, inc=1, device_id=(pipe + 1, me), device_id_type=MESH)

    def copy(src, dst, send_sem, recv_sem, to, along=None):
        return pltpu.make_async_remote_copy(
            src_ref=src,
            dst_ref=dst,
            send_sem=send_sem,
            recv_sem=recv_sem,
            device_id=(pipe if along is None else along, to),
            device_id_type=MESH,
        )

    def wait_for(ref, sem):
        pltpu.make_async_copy(ref, ref, sem).wait()

    def norm_of(x_ref, unit):
        def body(q, total):
            wide = x_ref[:, at(q, WIDTH)].astype(F32)
            return total + jnp.sum(wide * wide, axis=1, keepdims=True)

        total = lax.fori_loop(0, PARTS, body, jnp.zeros((TOK, 1), F32))
        unit[...] = jnp.broadcast_to(lax.rsqrt(total * (1.0 / D) + epsilon), unit.shape)

    fold_row = lax.div(lax.rem(iota((EXPERTS * TILE, 128), 0), TILE), 2)

    def dispatch(kind, slot, x_ref, table, unit, gate):
        def pack(q):
            values = x_ref[:, at(q, WIDTH)]
            if unit is not None:
                values = (values.astype(F32) * unit[:, 0:1]).astype(BF16)
            packed = dot(table, values)
            if gate is not None:
                packed = packed * gate
            left = jnp.zeros((EXPERTS * TILE, 128), F32)
            for b in range(BLOCKS):
                part_b = packed[EXPERTS * MAIN :, b * 128 : (b + 1) * 128]
                left = jnp.where(fold_row == b, part_b, left)
            for e in range(EXPERTS):
                to = e * PARTS + q
                snd[slot, at(to, MAIN), :] = packed[e * MAIN : (e + 1) * MAIN].astype(BF16)
                snd_fold[slot, at(to, TILE), :] = left[e * TILE : (e + 1) * TILE].astype(BF16)

        def send(to):
            copy(
                snd.at[slot, at(to, MAIN)], rows.at[kind, at(me, MAIN)], d_ss.at[slot], d_rs.at[kind], to
            ).start()
            copy(
                snd_fold.at[slot, at(to, TILE)], folds.at[kind, at(me, TILE)], d_sf.at[slot], d_rf.at[kind], to
            ).start()

        @pl.loop(1, PARTS)
        def _(s):
            q = (part + s) % PARTS
            pack(q)
            for r in range(EXPERTS):
                send(((mine + r) % EXPERTS) * PARTS + q)

        pack(part)
        for r in range(1, EXPERTS):
            send(((mine + r) % EXPERTS) * PARTS + part)
        rows[kind, at(me, MAIN), :] = snd[slot, at(me, MAIN), :]
        folds[kind, at(me, TILE), :] = snd_fold[slot, at(me, TILE), :]

    others_main = pl.ds(0, (PEERS - 1) * MAIN)
    others_fold = pl.ds(0, (PEERS - 1) * TILE)

    def sent(slot):
        wait_for(snd.at[slot, others_main], d_ss.at[slot])
        wait_for(snd_fold.at[slot, others_fold], d_sf.at[slot])

    def arrive(kind):
        wait_for(rows.at[kind, others_main], d_rs.at[kind])
        wait_for(folds.at[kind, others_fold], d_rf.at[kind])
        shape = (BLOCKS * ROWS_LEFT, FOLDED)
        to, come = iota(shape, 0), iota(shape, 1)
        place = lax.rem(to, ROWS_LEFT)
        wanted = lax.div(place, 2) * TILE + lax.div(to, ROWS_LEFT) * 2 + lax.rem(place, 2)
        spread = dot((come == wanted).astype(BF16), folds[kind])
        for b in range(BLOCKS):
            rows[kind, pl.ds(ROWS_MAIN, ROWS_LEFT), b * 128 : (b + 1) * 128] = spread[
                b * ROWS_LEFT : (b + 1) * ROWS_LEFT
            ].astype(BF16)

    def row_chunks(body):
        @pl.loop(0, 4)
        def _(i):
            body(at(i, 256), i)

        body(pl.ds(ROWS_MAIN, ROWS_LEFT), None)

    def step_1(kind, held):
        def body(chunk, _):
            lhs = rows[kind, chunk, :]
            for k in range(4):
                span = slice(k * 256, (k + 1) * 256)
                both = dot(lhs, q_down[span, :], NT) if kind == C else dot(lhs, q_up[:, span])
                low, high = both[:, :128], both[:, 128:]
                odd = core == 1
                keep[held, k, chunk, :] = jnp.where(odd, high, low)
                send1[kind, k, chunk, :] = jnp.where(odd, low, high).astype(BF16)

        row_chunks(body)
        copy(send1.at[kind], recv1.at[kind], h_s.at[kind], h_r.at[kind], other_core).start()

    def add_core(kind, held):
        wait_for(recv1.at[kind], h_r.at[kind])
        wait_for(send1.at[kind], h_s.at[kind])

        @pl.loop(0, 4)
        def _(k):
            keep[held, k] = keep[held, k] + recv1[kind, k].astype(F32)

    def half(kind, held, k, rows_at, to, step, come):
        total = keep[held, k, rows_at, :]
        if come:
            wait_for(passed.at[kind, k, rows_at], l_r.at[kind, k, step])
            total = total + passed[kind, k, rows_at, :].astype(F32)
        send1[kind, k, rows_at, :] = total.astype(BF16)
        copy(
            send1.at[kind, k, rows_at], passed.at[kind, k, rows_at], l_s.at[kind], l_r.at[kind, k, step], to
        ).start()

    def piece(n):
        return pl.ds(n % 2 * (ROWS // 2), ROWS // 2)

    def line_ends(kind, held):
        @pl.when(is_end)
        def _():
            for n in range(PIECES):
                half(kind, held, 2 - 2 * upper + n // 2, piece(n), over, n % 2, False)

    def line_mids(kind, held, n):
        @pl.when(jnp.logical_not(is_end))
        def _():
            if n < PIECES:
                half(kind, held, 2 - 2 * upper + n // 2, piece(n), over, n % 2, True)
            if n > 0:
                half(kind, held, 2 * upper + (n - 1) // 2, piece(n - 1), away, (n - 1) % 2, True)

    def line_come(kind, k, n):
        wait_for(passed.at[kind, k, piece(n)], l_r.at[kind, k, n % 2])

    def summed(kind, held, k, chunk):
        total = keep[held, k, chunk, :] + passed[kind, k, chunk, :].astype(F32)
        return total.astype(BF16).astype(F32)

    def hand(kind, k, n, to):
        span = gathered.at[kind, 2 * k + core, piece(n)]
        copy(span, span, g_s.at[kind], g_r.at[kind, k, n % 2], to).start()

    def hand_core(kind, k, n):
        span = gathered.at[kind, 2 * k + core, piece(n)]
        copy(span, span, c_s.at[kind], c_r.at[kind], other_core).start()

    def gather_own(kind, n):
        k = 2 * upper + n // 2
        hand(kind, k, n, over)
        hand_core(kind, k, n)

    def gather_mids(kind, n):
        @pl.when(jnp.logical_not(is_end))
        def _():
            for p, to in ((n, over), (n - 1, away)):
                if 0 <= p < PIECES:
                    k = (2 * upper if p == n else 2 - 2 * upper) + p // 2
                    wait_for(gathered.at[kind, 0, piece(p)], g_r.at[kind, k, p % 2])
                    hand(kind, k, p, to)
                    hand_core(kind, k, p)

    def gather_ends(kind):
        @pl.when(is_end)
        def _():
            for n in range(PIECES):
                k = 2 - 2 * upper + n // 2
                wait_for(gathered.at[kind, 0, piece(n)], g_r.at[kind, k, n % 2])
                hand_core(kind, k, n)

        wait_for(gathered.at[kind, pl.ds(0, 4)], c_r.at[kind])

    def wide(kind, chunk):
        return jnp.concatenate([gathered[kind, j, chunk, :] for j in range(PARTS)], axis=1)

    def give_back(slot, made):
        @pl.loop(0, 4)
        def _(i):
            snd[slot, at(i, 256), :] = made(at(i, 256)).astype(BF16)

        left = made(pl.ds(ROWS_MAIN, ROWS_LEFT)).astype(BF16)
        shape = (FOLDED, BLOCKS * ROWS_LEFT)
        to, come = iota(shape, 0), iota(shape, 1)
        inner = lax.rem(to, TILE)
        wanted = lax.div(inner, 2) * ROWS_LEFT + lax.div(to, TILE) * 2 + lax.rem(inner, 2)
        stacked = jnp.concatenate([left[:, b * 128 : (b + 1) * 128] for b in range(BLOCKS)], axis=0)
        snd_fold[slot] = dot((come == wanted).astype(BF16), stacked).astype(BF16)

        def send(to):
            copy(
                snd.at[slot, at(to, MAIN)], ret.at[slot, at(me, MAIN)], t_ss.at[slot], t_rs.at[slot, part], to
            ).start()
            copy(
                snd_fold.at[slot, at(to, TILE)], ret_fold.at[slot, at(me, TILE)],
                t_sf.at[slot], t_rf.at[slot, part], to,
            ).start()

        @pl.loop(1, PARTS)
        def _(s):
            for r in range(EXPERTS):
                send(((mine + r) % EXPERTS) * PARTS + (part + s) % PARTS)

        for r in range(1, EXPERTS):
            send(((mine + r) % EXPERTS) * PARTS + part)
        ret[slot, at(me, MAIN), :] = snd[slot, at(me, MAIN), :]
        ret_fold[slot, at(me, TILE), :] = snd_fold[slot, at(me, TILE), :]

    def come_back(slot, q, count):
        wait_for(ret.at[slot, pl.ds(0, count * MAIN)], t_rs.at[slot, q])
        wait_for(ret_fold.at[slot, pl.ds(0, count * TILE)], t_rf.at[slot, q])

    def combined(slot, q, mains, foldeds):
        come = jnp.concatenate([ret[slot, at(e * PARTS + q, MAIN), :] for e in range(EXPERTS)], axis=0)
        fold = jnp.concatenate([ret_fold[slot, at(e * PARTS + q, TILE), :] for e in range(EXPERTS)], axis=0)
        total = sum(dot(table, come) for table in mains)
        extra = sum(dot(table, fold) for table in foldeds)
        return total + jnp.concatenate([extra[b * TOK : (b + 1) * TOK] for b in range(BLOCKS)], axis=1)

    by_row = jnp.concatenate(
        (routes_a[...].astype(F32), gates_a[...], routes_b[...].astype(F32), gates_b[...]), axis=0
    )
    same = (iota((TOK, TOK), 0) == iota((TOK, TOK), 1)).astype(BF16)
    by_col = sum(dot(same, term, NT) for term in terms(by_row, 3))
    table_b, gate_b = pack_tables(by_row[4:6], by_row[6:8])
    norm_of(xb, unit_b)
    pl.semaphore_wait(
        barrier, PEERS - 1 + jnp.where(pipe > 0, 1, 0) + jnp.where(pipe < N_PIPE - 1, 1, 0)
    )
    dispatch(U, 0, xb, table_b, unit_b, None)
    loads[0].wait()
    dispatch(C, 1, cb, table_b, None, gate_b)

    for load in loads[1:]:
        load.wait()

    step_up, step_down = s_up[0, mine], s_down[0, mine]
    one = jnp.ones((1, 1), F32)
    inv_up, inv_down = one / step_up, one / step_down

    @pl.loop(0, WIDTH // 64)
    def _(i):
        ratio, _, _, bend = waves(w_up[at(i, 64), :], inv_up)
        q_up[at(i, 64), :] = (step_up * (ratio - bend)).astype(BF16)

    @pl.loop(0, HID // 64)
    def _(i):
        ratio, _, _, bend = waves(w_down[at(i, 64), :], inv_down)
        q_down[at(i, 64), :] = (step_down * (ratio - bend)).astype(BF16)

    table_a, _ = pack_tables(by_row[0:2], by_row[2:4])
    norm_of(xa, unit_a)

    arrive(U)
    step_1(U, 0)
    sent(0)
    dispatch(A, 0, xa, table_a, unit_a, None)
    arrive(C)
    step_1(C, 1)
    add_core(U, 0)
    line_ends(U, 0)
    add_core(C, 1)
    line_ends(C, 1)
    for n in range(PIECES + 1):
        line_mids(U, 0, n)
        line_mids(C, 1, n)

    @pl.when(is_end)
    def _():
        for n in range(PIECES):
            k = 2 * upper + n // 2
            chunk = piece(n)
            line_come(U, k, n)
            line_come(C, k, n)
            pre = summed(U, 0, k, chunk)
            grad = summed(C, 1, k, chunk)
            sigma = 1.0 / (1.0 + jnp.exp(-pre))
            gathered[U, 2 * k + core, chunk, :] = (grad * (sigma * (1.0 + pre * (1.0 - sigma)))).astype(BF16)
            gathered[C, 2 * k + core, chunk, :] = (pre * sigma).astype(BF16)
            gather_own(U, n)
            gather_own(C, n)

    arrive(A)
    step_1(A, 0)
    for n in range(2):
        gather_mids(U, n)
        gather_mids(C, n)
    add_core(A, 0)
    line_ends(A, 0)
    for n in range(2, PIECES + 1):
        gather_mids(U, n)
        gather_mids(C, n)
    for n in range(PIECES + 1):
        line_mids(A, 0, n)
    gather_ends(U)
    sent(1)
    give_back(1, lambda chunk: dot(wide(U, chunk), q_up[...], NT))

    @pl.when(is_end)
    def _():
        for n in range(PIECES):
            k = 2 * upper + n // 2
            chunk = piece(n)
            line_come(A, k, n)
            pre = summed(A, 0, k, chunk)
            gathered[A, 2 * k + core, chunk, :] = (pre / (1.0 + jnp.exp(-pre))).astype(BF16)
            gather_own(A, n)

    for n in range(PIECES + 1):
        gather_mids(A, n)
    gather_ends(C)
    gather_ends(A)
    sent(0)
    give_back(0, lambda chunk: dot(wide(A, chunk), q_down[...]))

    def quant_grads(weights, inverse, grads):
        ratio, inside, sine, bend = waves(weights, inverse)
        wave = jnp.where(inside, 2.0 * sine * sine, 0.0)
        grads = grads.astype(BF16).astype(F32)
        return (grads * wave).astype(BF16), jnp.sum(
            grads * (ratio - bend - ratio * wave), axis=0, keepdims=True
        )

    def up_step(i):
        lhs = rows[U, :, at(i, 128)]
        for k in range(4):
            rhs = jnp.concatenate([gathered[U, 2 * k], gathered[U, 2 * k + 1]], axis=1)
            span = slice(k * 256, (k + 1) * 256)
            out, partial = quant_grads(w_up[at(i, 128), span], inv_up, dot(lhs, rhs, TN))
            o_up[at(i, 128), span] = out
            up_total[:, span] = up_total[:, span] + partial

    def down_step(j):
        out, partial = quant_grads(w_down[at(j, 128), :], inv_down, dot(gathered[C, j], rows[C], TN))
        o_down[at(j, 128), :] = out
        down_total[...] = down_total[...] + partial

    up_total[...] = jnp.zeros_like(up_total)
    down_total[...] = jnp.zeros_like(down_total)

    @pl.loop(4, BLOCKS)
    def _(i):
        up_step(i)

    main_b, fold_b = unpack_tables(by_col[:, 4:6], None)
    main_b, fold_b = terms(main_b, 1), terms(fold_b, 1)

    def take_b(q):
        grads = combined(1, q, main_b, fold_b)
        g_wide[:, at(q, WIDTH)] = grads
        return jnp.sum(xb[:, at(q, WIDTH)].astype(F32) * grads, axis=1, keepdims=True)

    def body_b(s, total):
        q = (part + PARTS - s) % PARTS
        come_back(1, q, EXPERTS)
        return total + take_b(q)

    along = lax.fori_loop(1, PARTS, body_b, jnp.zeros((TOK, 1), F32))
    come_back(1, part, EXPERTS - 1)
    along = along + take_b(part)
    unit = unit_b[:, 0:1]
    bent = along * unit * unit * unit * (1.0 / D)

    @pl.loop(0, PARTS)
    def _(q):
        span = at(q, WIDTH)
        back = g_wide[:, span] * unit - xb[:, span].astype(F32) * bent
        out_b[:, span] = (cb[:, span].astype(F32) + back).astype(BF16)

        @pl.when(pipe > 0)
        def _():
            copy(out_b.at[:, span], o_cot.at[:, span], p_s.at[1], p_r.at[1], me, pipe - 1).start()

    main_a, fold_a = unpack_tables(by_col[:, 0:2], by_col[:, 2:4])
    main_a, fold_a = terms(main_a, 3), terms(fold_a, 3)

    def take_a(q):
        span = at(q, WIDTH)
        out_a[:, span] = (xa[:, span].astype(F32) + combined(0, q, main_a, fold_a)).astype(BF16)

        @pl.when(pipe < N_PIPE - 1)
        def _():
            copy(out_a.at[:, span], o_next.at[:, span], p_s.at[0], p_r.at[0], me, pipe + 1).start()

    @pl.loop(1, 5)
    def _(s):
        up_step(s - 1)
        down_step(2 * s - 2)
        down_step(2 * s - 1)
        q = (part + PARTS - s) % PARTS
        come_back(0, q, EXPERTS)
        take_a(q)

    stores = [pltpu.make_async_copy(o_up, up_to, o_s.at[0]), pltpu.make_async_copy(o_down, down_to, o_s.at[1])]
    for store in stores:
        store.start()
    first = iota((8, 128), 0) == 0
    scaled = 1.0 / math.sqrt(D * HID * qlimit)
    sum_snd[...] = (
        jnp.where(
            first,
            jnp.sum(up_total[...], axis=1, keepdims=True),
            jnp.sum(down_total[...], axis=1, keepdims=True),
        )
        * scaled
    )
    sum_rcv[me] = sum_snd[...]

    @pl.loop(1, PEERS)
    def _(i):
        copy(sum_snd, sum_rcv.at[me], z_s, z_r, (me + i) % PEERS).start()

    @pl.loop(5, PARTS)
    def _(s):
        q = (part + PARTS - s) % PARTS
        come_back(0, q, EXPERTS)
        take_a(q)

    come_back(0, part, EXPERTS - 1)
    take_a(part)

    wait_for(sum_rcv.at[pl.ds(0, PEERS - 1)], z_r)
    lane = iota((8, 128), 1)
    sums = jnp.zeros((8, 128), F32)
    for e in range(EXPERTS):
        sums = jnp.where(lane == e, sum(sum_rcv[e * PARTS + k] for k in range(PARTS)), sums)
    o_up_sums[...] = sums[0:1, :EXPERTS]
    o_down_sums[...] = sums[1:2, :EXPERTS]

    wait_for(sum_rcv.at[pl.ds(0, PEERS - 1)], z_s)
    for store in stores:
        store.wait()
    for slot in (0, 1):
        wait_for(snd.at[slot, others_main], t_ss.at[slot])
        wait_for(snd_fold.at[slot, others_fold], t_sf.at[slot])
    for kind in (U, C, A):
        wait_for(gathered.at[kind, pl.ds(0, 4)], c_s.at[kind])

        @pl.when(is_end)
        def _():
            wait_for(send1.at[kind, pl.ds(0, 2)], l_s.at[kind])
            wait_for(gathered.at[kind, pl.ds(0, 2)], g_s.at[kind])

        @pl.when(jnp.logical_not(is_end))
        def _():
            wait_for(send1.at[kind], l_s.at[kind])
            wait_for(gathered.at[kind, pl.ds(0, 4)], g_s.at[kind])

    @pl.when(pipe > 0)
    def _():
        wait_for(out_b, p_s.at[1])
        wait_for(o_next, p_r.at[0])

    @pl.when(pipe == 0)
    def _():
        o_next[...] = jnp.zeros_like(o_next)

    @pl.when(pipe < N_PIPE - 1)
    def _():
        wait_for(out_a, p_s.at[0])
        wait_for(o_cot, p_r.at[1])

    @pl.when(pipe == N_PIPE - 1)
    def _():
        o_cot[...] = jnp.zeros_like(o_cot)


def shards(
    acts_a, acts_b, cot_b, routes_a, gates_a, routes_b, gates_b, up_weight, down_weight, up_scale, down_scale
):
    vmem = pl.BlockSpec(memory_space=pltpu.VMEM)
    hbm = pl.BlockSpec(memory_space=pl.ANY)
    smem = pl.BlockSpec(memory_space=pltpu.SMEM)
    dma = pltpu.SemaphoreType.DMA

    def bf(*shape):
        return pltpu.VMEM(shape, BF16)

    def wide(*shape):
        return pltpu.VMEM(shape, F32)

    def out(*shape):
        return jax.ShapeDtypeStruct(shape, BF16)

    made = pl.pallas_call(
        kernel,
        out_shape=(
            out(TOK, D), out(TOK, D), out(WIDTH, HID), out(HID, WIDTH),
            jax.ShapeDtypeStruct((1, EXPERTS), F32), jax.ShapeDtypeStruct((1, EXPERTS), F32),
        ),
        in_specs=[hbm, vmem, hbm, vmem, vmem, vmem, vmem, hbm, hbm, smem, smem],
        out_specs=(vmem, vmem, hbm, hbm, vmem, vmem),
        scratch_shapes=[
            bf(TOK, D), bf(TOK, D), bf(WIDTH, HID), bf(HID, WIDTH), bf(WIDTH, HID), bf(HID, WIDTH),
            dma((4,)), dma((2,)),
            bf(WIDTH, HID), bf(HID, WIDTH),
            bf(3, ROWS, WIDTH), bf(3, FOLDED, 128),
            bf(2, ROWS_MAIN, WIDTH), bf(2, FOLDED, 128),
            bf(2, ROWS_MAIN, WIDTH), bf(2, FOLDED, 128),
            wide(2, 4, ROWS, 128),
            bf(3, 4, ROWS, 128), bf(3, 4, ROWS, 128),
            bf(3, 4, ROWS, 128),
            bf(3, PARTS, ROWS, 128),
            bf(TOK, D), bf(TOK, D), wide(TOK, D),
            wide(TOK, 128), wide(TOK, 128),
            wide(1, HID), wide(1, WIDTH), wide(8, 128), wide(PEERS, 8, 128),
            dma((2,)), dma((3,)), dma((2,)), dma((3,)),
            dma((3,)), dma((3,)), dma((3,)), dma((3, 4, 2)), dma((3,)), dma((3, 4, 2)), dma((3,)), dma((3,)),
            dma((2,)), dma((2, PARTS)), dma((2,)), dma((2, PARTS)),
            dma((2,)), dma((2,)), dma, dma,
        ],
        compiler_params=pltpu.CompilerParams(
            collective_id=0, has_side_effects=True, vmem_limit_bytes=62 << 20
        ),
    )(
        acts_a[0], acts_b[0], cot_b[0], routes_a[0].T, gates_a[0].T, routes_b[0].T, gates_b[0].T, up_weight[0], down_weight[0], up_scale, down_scale
    )
    next_a, next_cot, dw_up, dw_down, up_sums, down_sums = made
    return (next_a[None], next_cot[None], dw_up[None], dw_down[None], up_sums, down_sums)


def solution(mesh):
    split, rows = P("pipe", "expert", None), P("pipe", None)
    columns = P("pipe", None, "expert")
    return jax.shard_map(
        shards,
        mesh=mesh,
        in_specs=(split,) * 8 + (columns, rows, rows),
        out_specs=(split, split, split, columns, rows, rows),
        check_vma=False,
    )
```
